256 devices in a mesh: space: 16 (over x, y_hi, core), replica: 16 (over z, y_lo).
Axes of the slice: x: 4, y: 4 (y_hi: 2, y_lo: 2; y = y_hi * 2 + y_lo), z: 8, core: 2. Of those that a mesh axis runs over, the one named last changes fastest.
Arguments:
- activations: bfloat16 [16, 32, 64, 48, 256], P('replica', None, 'space'), may hold values from -6 to 6
- preact: bfloat16 [16, 32, 32, 24, 128], P('replica', None, 'space'), may hold values from -6 to 6
- cotangent: bfloat16 [16, 32, 32, 24, 128], P('replica', None, 'space'), may hold values from -0.01171875 to 0.01171875
- conv_weight: bfloat16 [27, 32, 32], replicated, may hold values from -0.21875 to 0.21875
Outputs:
- weight_grads: float32 [2, 27648], P(None, 'space')
The draws below stay inside these ranges and needn't reach their ends.
All inputs are finite; a program needn't handle non-finite values.
Results may differ from the reference program's by a relative error of at most 0.003.
Values may be sent and summed in bfloat16 or wider, within the bound.
No kernel may reach another device: no remote copies, remote signals or barrier semaphores. Data moves between devices by JAX's collectives and lax.ppermute only.
A program may use at most 128 MiB of HBM per device.

```python
import jax
import jax.numpy as jnp
from jax import lax

C = 32
NZ = 48
NY = 256
REPLICAS = 16
NX = 64
N_REPLICA = 16


def shard_levels(stream_key, dims, shards, smallest, top_value):
    level, own = 1.0, jax.random.fold_in(stream_key, 6)
    for dim, parts in shards:
        heights = jnp.exp(jax.random.uniform(jax.random.fold_in(own, dim), (parts,), jnp.float32, smallest / len(shards), top_value / len(shards)))
        level = level * jnp.repeat(heights, dims[dim] // parts).reshape([-1 if axis == dim else 1 for axis in range(len(dims))])
    return level


def scatter_about(stream_key, shape, deviation, limit, cuts=(), kind=jnp.bfloat16):
    entries = jax.random.normal(stream_key, shape, jnp.float32) * deviation
    if len(cuts) > 0:
        entries = shard_levels(stream_key, shape, cuts, -0.22, 0.18) * entries
    return jnp.clip(entries, min=-limit, max=limit).astype(kind)


def setup_inputs(seed: int = 0) -> dict:
    keys = jax.random.split(jax.random.key(seed), 5)
    activations = scatter_about(keys[0], (REPLICAS, C, NX, NZ, NY), 1.0, 6.0, ((0, 16), (2, 16)))
    preact = scatter_about(keys[1], (REPLICAS, C, NX // 2, NZ // 2, NY // 2), 1.5, 6.0, ((0, 16), (2, 16)))
    cotangent = scatter_about(keys[2], (REPLICAS, C, NX // 2, NZ // 2, NY // 2), ((N_REPLICA * NX * NZ * NY // 8) ** -0.5), 0.01171875, ((0, 16), (2, 16)))
    conv_weight = scatter_about(keys[3], (27, C, C), (27 * C) ** -0.5, 0.21875)
    return {"activations": activations, "preact": preact, "cotangent": cotangent, "conv_weight": conv_weight}


def section_terms(act_pad, cot_pad, preact, conv_weight):
    channels, out_x, out_z, out_y = preact.shape
    volume = out_x * out_z * out_y
    pre_float = preact.astype(jnp.float32).reshape(channels, volume)
    hidden = jax.nn.silu(pre_float).astype(jnp.bfloat16)
    hidden_grad = jnp.zeros((channels, volume), jnp.float32)
    grads_second = []
    tap_index = 0
    for step_x in range(3):
        for step_z in range(3):
            for step_y in range(3):
                cot_slice = cot_pad[:, 2 - step_x:2 - step_x + out_x, 2 - step_z:2 - step_z + out_z, 2 - step_y:2 - step_y + out_y].reshape(channels, volume)
                hidden_grad = hidden_grad + jnp.dot(conv_weight[tap_index].T, cot_slice, preferred_element_type=jnp.float32)
                grads_second.append(lax.dot_general(cot_slice, hidden, (((1,), (1,)), ((), ())), preferred_element_type=jnp.float32))
                tap_index = tap_index + 1
    gate_val = jax.nn.sigmoid(pre_float)
    pre_grad = (hidden_grad * gate_val * (1.0 + pre_float * (1.0 - gate_val))).astype(jnp.bfloat16)
    grads_first = []
    for step_x in range(3):
        for step_z in range(3):
            for step_y in range(3):
                act_slice = act_pad[:, step_x:step_x + 2 * out_x - 1:2, step_z:step_z + 2 * out_z - 1:2, step_y:step_y + 2 * out_y - 1:2].reshape(channels, volume)
                grads_first.append(lax.dot_general(pre_grad, act_slice, (((1,), (1,)), ((), ())), preferred_element_type=jnp.float32))
    return jnp.stack([jnp.stack(grads_first), jnp.stack(grads_second)]).reshape(2, -1)


def reference(activations, preact, cotangent, conv_weight):
    def one_replica(items):
        volume_in, pre_one, cot_one = items
        act_pad = jnp.pad(volume_in, ((0, 0), (1, 0), (1, 0), (1, 0)))
        cot_pad = jnp.pad(cot_one, ((0, 0), (1, 1), (1, 1), (1, 1)))
        return section_terms(act_pad, cot_pad, pre_one, conv_weight)

    stacked = lax.map(one_replica, (activations, preact, cotangent))
    return jnp.sum(stacked, axis=0, dtype=jnp.float32)
```

```python
import jax
import jax.numpy as jnp
from jax import lax
from jax.experimental import pallas as pl
from jax.experimental.pallas import tpu as pltpu
from jax.sharding import PartitionSpec as P

BF = jnp.bfloat16
F32 = jnp.float32

C = 32
QX, QZ, QY = 2, 24, 128
IX, IZ, IY = 4, 48, 256
TAPS2 = 288
TAPS1 = 96

NT = (((1,), (1,)), ((), ()))


def relaid(flat_ref, step, stride):
    return flat_ref[pl.ds(step, C, stride=stride), :]


def section_kernel(
    act_ref, act_prev_ref, cot_ref, cot_prev_ref, cot_next_ref, pre_ref, weight_ref,
    out_ref,
    flat_act, flat_small, act_t, cot_t, pre_t, hidden_t, weight_t, second_acc, first_acc, flips, dense,
):
    act_t[:, 0:C, :] = jnp.zeros((IX + 1, C, IY), BF)
    cot_t[:, 0:C, :] = jnp.zeros((QX + 2, C, QY), BF)
    cot_t[:, (QZ + 1) * C : (QZ + 2) * C, :] = jnp.zeros((QX + 2, C, QY), BF)

    for plane in range(IX + 1):
        block = act_prev_ref[...] if plane == 0 else act_ref[:, plane - 1]
        flat = block.astype(F32).reshape(C * IZ, IY)
        for side in range(2):
            flat_act[plane % 2, side] = flat[:, side * 128 : (side + 1) * 128]

        def move_act(z, carry, plane=plane):
            start = pl.multiple_of((z + 1) * C, C)
            for side in range(2):
                tile = relaid(flat_act.at[plane % 2, side], z, IZ).astype(BF)
                act_t[plane, pl.ds(start, C), side * 128 : (side + 1) * 128] = tile
            return carry

        lax.fori_loop(0, IZ, move_act, 0, unroll=8)

    for plane in range(QX + 2):
        if plane == 0:
            block = cot_prev_ref[...]
        elif plane == QX + 1:
            block = cot_next_ref[...]
        else:
            block = cot_ref[:, plane - 1]
        flat_small[plane] = block.astype(F32).reshape(C * QZ, QY)
    for plane in range(QX):
        flat_small[QX + 2 + plane] = pre_ref[:, plane].astype(F32).reshape(C * QZ, QY)

    lanes = lax.broadcasted_iota(jnp.int32, (C, QY), 1)

    def shifted(x, by):
        edge = 0 if by == 1 else QY - 1
        return jnp.where(lanes == edge, 0.0, pltpu.roll(x, by % QY, 1))

    for plane in range(QX + 2):

        def move_cot(z, carry, plane=plane):
            start = pl.multiple_of((z + 1) * C, C)
            cot_t[plane, pl.ds(start, C), :] = relaid(flat_small.at[plane], z, QZ).astype(BF)
            return carry

        lax.fori_loop(0, QZ, move_cot, 0, unroll=8)

    for plane in range(QX):

        def move_pre(z, carry, plane=plane):
            pre = relaid(flat_small.at[QX + 2 + plane], z, QZ)
            gate = jax.nn.sigmoid(pre)
            hidden = (pre * gate).astype(BF).astype(F32)
            hidden_t[plane, z] = jnp.concatenate(
                [shifted(hidden, 1), hidden, shifted(hidden, -1)], axis=0
            ).astype(BF)
            pre_t[plane, z] = gate * (1.0 + pre * (1.0 - gate))
            return carry

        lax.fori_loop(0, QZ, move_pre, 0, unroll=4)

    for j in range(3):
        for k in range(3):
            base = (2 - j) * 9 + (2 - k) * 3
            wide = jnp.concatenate([weight_ref[base + d].astype(F32) for d in range(3)], axis=1)
            weight_t[(j * 3 + k) * C : (j * 3 + k + 1) * C, :] = wide
    weights = weight_t[...].T.astype(BF)

    row = lax.broadcasted_iota(jnp.int32, (QY, 3 * IY), 0)
    col = lax.broadcasted_iota(jnp.int32, (QY, 3 * IY), 1)
    spread = jnp.where(col % IY == 2 * row + col // IY - 1, 1.0, 0.0).astype(BF)

    second_acc[...] = jnp.zeros((TAPS2, TAPS1), F32)
    first_acc[...] = jnp.zeros((TAPS2, TAPS1), F32)

    def pair_step(pair, carry):
        for x in range(QX):
            slabs = []
            for half in range(2):
                z = pair * 2 + half
                start = pl.multiple_of(z * C, C)
                slabs.append(
                    jnp.concatenate([cot_t[x + j, pl.ds(start, 3 * C), :] for j in range(3)], axis=0)
                )
            slab = jnp.concatenate(slabs, axis=1)
            hid = jnp.concatenate([hidden_t[x, pair * 2], hidden_t[x, pair * 2 + 1]], axis=1)
            second_acc[...] += lax.dot_general(slab, hid, NT, preferred_element_type=F32)
            terms = jnp.dot(weights, slab, preferred_element_type=F32)
            rows = []
            for half in range(2):
                part = terms[:, half * QY : (half + 1) * QY]
                hidden_grad = part[C : 2 * C] + shifted(part[0:C], -1) + shifted(part[2 * C :], 1)
                rows.append((hidden_grad * pre_t[x, pair * 2 + half]).astype(BF))
            grads = jnp.concatenate(rows, axis=0)
            wide = jnp.dot(grads, spread, preferred_element_type=F32).astype(BF)
            for half in range(2):
                z = pair * 2 + half
                ups = jnp.concatenate(
                    [wide[half * C : (half + 1) * C, d * IY : (d + 1) * IY] for d in range(3)], axis=0
                )
                start = pl.multiple_of(z * 2 * C, C)
                acts = jnp.concatenate(
                    [act_t[2 * x + a, pl.ds(start, 3 * C), :] for a in range(3)], axis=0
                )
                first_acc[...] += lax.dot_general(acts, ups, NT, preferred_element_type=F32)
        return carry

    lax.fori_loop(0, QZ // 2, pair_step, 0)

    first_flip = first_acc[...].T
    for side in range(3):
        wide = min(128, TAPS2 - side * 128)
        flips[side, 0:TAPS1, 0:wide] = first_flip[:, side * 128 : side * 128 + wide]
    flips[3, :, 0:TAPS1] = second_acc[...]
    lane = lax.broadcasted_iota(jnp.int32, (8, 128), 1)
    for ab in range(9):
        ab_rev = (2 - ab // 3) * 3 + (2 - ab % 3)
        for d in range(3):
            for which in range(2):
                total = jnp.zeros((8, 128), F32)
                for r in range(4):
                    if which == 0:
                        side, offset, begin = ab // 4, (ab % 4) * C, d * C + r
                    else:
                        side, offset, begin = 3, d * C, ab_rev * C + r
                    part = flips[side, pl.ds(begin, 8, stride=4), :]
                    turn = (r * C - offset) % 128
                    part = pltpu.roll(part, turn, 1) if turn else part
                    total = jnp.where(lane // C == r, part, total)
                dense[which, (ab * 3 + d) * 8 : (ab * 3 + d + 1) * 8, :] = total

    for s in range(16):
        begin = (27 * s) // 2
        for which in range(2):
            out_ref[s, which, 0:14, :] = dense[which, begin : begin + 14, :]
            out_ref[s, which, 14:16, :] = jnp.zeros((2, 128), F32)


def section_terms(act, act_prev, cot, cot_prev, cot_next, pre, weight):
    vmem = pl.BlockSpec(memory_space=pltpu.VMEM)
    return pl.pallas_call(
        section_kernel,
        out_shape=jax.ShapeDtypeStruct((16, 2, 16, 128), F32),
        in_specs=[vmem] * 7,
        out_specs=vmem,
        scratch_shapes=[
            pltpu.VMEM((2, 2, C * IZ, 128), F32),
            pltpu.VMEM((2 * QX + 2, C * QZ, QY), F32),
            pltpu.VMEM((IX + 1, (IZ + 1) * C, IY), BF),
            pltpu.VMEM((QX + 2, (QZ + 2) * C, QY), BF),
            pltpu.VMEM((QX, QZ, C, QY), F32),
            pltpu.VMEM((QX, QZ, TAPS1, QY), BF),
            pltpu.VMEM((TAPS2, TAPS1), F32),
            pltpu.VMEM((TAPS2, TAPS1), F32),
            pltpu.VMEM((TAPS2, TAPS1), F32),
            pltpu.VMEM((4, TAPS2, 128), F32),
            pltpu.VMEM((2, 216, 128), F32),
        ],
        compiler_params=pltpu.CompilerParams(vmem_limit_bytes=48 * 2**20),
        name="section_terms",
    )(act, act_prev, cot, cot_prev, cot_next, pre, weight)


def moved(x, axis, by):
    length = lax.axis_size(axis)
    pairs = [(i, i + by) for i in range(length) if 0 <= i + by < length]
    return lax.ppermute(x, axis, pairs)


def on_device(activations, preact, cotangent, conv_weight):
    act, pre, cot = activations[0], preact[0], cotangent[0]
    cot_prev = moved(cot[:, QX - 1], "space", 1)
    cot_next = moved(cot[:, 0], "space", -1)
    act_prev = moved(act[:, IX - 1], "space", 1)
    terms = section_terms(act, act_prev, cot, cot_prev, cot_next, pre, conv_weight)
    shares = lax.all_to_all(terms, "space", 0, 0, tiled=True)
    share = jnp.sum(shares, axis=0)
    copies = lax.all_to_all(jnp.broadcast_to(share[None], (16, 2, 16, 128)), "replica", 0, 0, tiled=True)
    total = jnp.sum(copies, axis=0)[:, :14].reshape(2, 14 * 128)
    odd = lax.axis_index("space") % 2
    return lax.dynamic_slice(total, (0, 64 * odd), (2, 1728))


def solution(mesh):
    return jax.shard_map(
        on_device,
        mesh=mesh,
        in_specs=(
            P("replica", None, "space", None, None),
            P("replica", None, "space", None, None),
            P("replica", None, "space", None, None),
            P(),
        ),
        out_specs=P(None, "space"),
        check_vma=False,
    )
```

```python
import jax
import jax.numpy as jnp
from jax import lax
from jax.experimental import pallas as pl
from jax.experimental.pallas import tpu as pltpu
from jax.sharding import Mesh, PartitionSpec as P

BF = jnp.bfloat16
F32 = jnp.float32

C = 32
QX, QZ, QY = 2, 24, 128
IX, IZ, IY = 4, 48, 256
T3 = 3 * C
COT_ROWS = (QZ + 3) * C
ACT_ROWS = (IZ + 1) * C
TAPS = 9 * C

NT = (((1,), (1,)), ((), ()))


def nt_dot(a, b):
    return lax.dot_general(a, b, NT, preferred_element_type=F32)


def lane_shift(x, by):
    lanes = lax.broadcasted_iota(jnp.int32, x.shape, 1)
    return jnp.where(lanes == (0 if by == 1 else QY - 1), 0.0, pltpu.roll(x, by % QY, 1))


def taps_joined(part):
    return part[C : 2 * C] + lane_shift(part[0:C], -1) + lane_shift(part[2 * C : T3], 1)


def four_blocks(rows):
    return jnp.concatenate([rows, rows[0:C]], axis=0)


def cot_kernel(cot_ref, first_ref, last_ref, flat):
    for plane, out_ref in ((0, first_ref), (1, last_ref)):
        flat[plane] = cot_ref[:, plane].astype(F32).reshape(C * QZ, QY)
        out_ref[0:C, :] = jnp.zeros((C, QY), BF)
        out_ref[(QZ + 1) * C :, :] = jnp.zeros((2 * C, QY), BF)
        for z in range(QZ):
            block = flat[plane, pl.ds(z, C, stride=QZ), :]
            out_ref[(z + 1) * C : (z + 2) * C, :] = block.astype(BF)


def local_kernel(
    act_ref, pre_ref, weight_ref, cot0_ref, cot1_ref,
    act_t, hidden_t, scale_t, partial_t, rim_weights, spread_ref, second_ref,
    flat_act, flat_pre, weight_t,
):
    for j in range(3):
        for k in range(3):
            base = (2 - j) * 9 + (2 - k) * 3
            wide = jnp.concatenate([weight_ref[base + d].astype(F32) for d in range(3)], axis=1)
            weight_t[(j * 4 + k) * C : (j * 4 + k + 1) * C, 0:T3] = wide
        weight_t[(j * 4 + 3) * C : (j * 4 + 4) * C, :] = jnp.zeros((C, 128), F32)
    flipped = [weight_t[j * 128 : (j + 1) * 128, 0:T3].T.astype(BF) for j in range(3)]
    rim_weights[0] = flipped[0]
    rim_weights[1] = flipped[2]
    weights = jnp.concatenate(
        [
            jnp.concatenate([flipped[1], flipped[2]], axis=1),
            jnp.concatenate([flipped[0], flipped[1]], axis=1),
        ],
        axis=0,
    )

    row = lax.broadcasted_iota(jnp.int32, (QY, 3 * IY), 0)
    col = lax.broadcasted_iota(jnp.int32, (QY, 3 * IY), 1)
    spread_ref[...] = jnp.where(col % IY == 2 * row + col // IY - 1, 1.0, 0.0).astype(BF)

    for plane in range(QX):
        flat_pre[plane] = pre_ref[:, plane].astype(F32).reshape(C * QZ, QY)
        for z in range(QZ):
            pre = flat_pre[plane, pl.ds(z, C, stride=QZ), :]
            gate = jax.nn.sigmoid(pre)
            hidden = (pre * gate).astype(BF).astype(F32)
            hidden_t[plane, z * T3 : (z + 1) * T3, :] = jnp.concatenate(
                [lane_shift(hidden, 1), hidden, lane_shift(hidden, -1)], axis=0
            ).astype(BF)
            scale_t[plane, z * C : (z + 1) * C, :] = gate * (1.0 + pre * (1.0 - gate))

    for plane in range(IX):
        act_t[plane, 0:C, :] = jnp.zeros((C, IY), BF)
        flat = act_ref[:, plane].astype(F32).reshape(C * IZ, IY)
        for side in range(2):
            flat_act[plane % 2, side] = flat[:, side * 128 : (side + 1) * 128]
        for z in range(IZ):
            for side in range(2):
                tile = flat_act[plane % 2, side, pl.ds(z, C, stride=IZ), :].astype(BF)
                act_t[plane, (z + 1) * C : (z + 2) * C, side * 128 : (side + 1) * 128] = tile

    for z in range(0, QZ, 2):
        slab = jnp.concatenate(
            [
                jnp.concatenate([ref[(z + h) * C : (z + h + 4) * C, :] for h in range(2)], axis=1)
                for ref in (cot0_ref, cot1_ref)
            ],
            axis=0,
        )
        terms = jnp.dot(weights, slab, preferred_element_type=F32)
        for x in range(QX):
            for h in range(2):
                part = terms[x * T3 : (x + 1) * T3, h * QY : (h + 1) * QY]
                partial_t[x, (z + h) * C : (z + h + 1) * C, :] = taps_joined(part)

    total = jnp.zeros((2 * T3, 256), F32)
    for z0 in range(0, QZ, 8):
        slab = jnp.concatenate(
            [
                jnp.concatenate([ref[z * C : (z + 3) * C, :] for z in range(z0, z0 + 8)], axis=1)
                for ref in (cot0_ref, cot1_ref)
            ],
            axis=0,
        )
        hid = jnp.concatenate(
            [
                jnp.concatenate(
                    [four_blocks(hidden_t[x, z * T3 : (z + 1) * T3, :]) for x in range(QX)], axis=0
                )
                for z in range(z0, z0 + 8)
            ],
            axis=1,
        )
        total = total + nt_dot(slab, hid)
    second_ref[0:T3, :] = total[0:T3, 128:256]
    second_ref[T3 : 2 * T3, :] = total[0:T3, 0:128] + total[T3:, 128:256]
    second_ref[2 * T3 :, :] = total[T3:, 0:128]


def pre_grads(cot_ref, weights, partial, scale, put):
    for z in range(0, QZ, 2):
        slab = jnp.concatenate([cot_ref[(z + h) * C : (z + h + 4) * C, :] for h in range(2)], axis=1)
        terms = jnp.dot(weights, slab, preferred_element_type=F32)
        for h in range(2):
            rows = slice((z + h) * C, (z + h + 1) * C)
            grad = partial[rows, :] + taps_joined(terms[:, h * QY : (h + 1) * QY])
            put(rows, (grad * scale[rows, :]).astype(BF))


def rim_kernel(cot_prev_ref, rim_weights, partial_ref, scale_ref, out_ref):
    def put(rows, value):
        out_ref[rows, :] = value

    pre_grads(cot_prev_ref, rim_weights[0], partial_ref.at[0], scale_ref.at[0], put)


def spread_plane(grad_ref, spread_ref, wide_ref):
    for z0 in range(0, QZ, 4):
        wide = jnp.dot(
            grad_ref[z0 * C : (z0 + 4) * C, :], spread_ref[...], preferred_element_type=F32
        ).astype(BF)
        for h in range(4):
            for d in range(3):
                begin = (z0 + h) * T3 + d * C
                wide_ref[begin : begin + C, :] = wide[h * C : (h + 1) * C, d * IY : (d + 1) * IY]


def main_kernel(
    cot_prev_ref, cot_next_ref, rim_weights, partial_ref, scale_ref, hidden_t, act_t, grad0_ref,
    spread_ref, second_in,
    first_ref, second_ref,
    grad1, wide, acc,
):
    def put(rows, value):
        grad1[rows, :] = value

    pre_grads(cot_next_ref, rim_weights[1], partial_ref.at[1], scale_ref.at[1], put)
    spread_plane(grad0_ref, spread_ref, wide.at[0])
    spread_plane(grad1, spread_ref, wide.at[1])

    second_ref[T3 : 2 * T3, :] = second_in[T3 : 2 * T3, :]
    for x, ref in ((0, cot_prev_ref), (1, cot_next_ref)):
        rows = slice(2 * x * T3, (2 * x + 1) * T3)
        total = second_in[rows, :]
        for z0 in range(0, QZ, 8):
            slab = jnp.concatenate([ref[z * C : (z + 3) * C, :] for z in range(z0, z0 + 8)], axis=1)
            hid = jnp.concatenate(
                [four_blocks(hidden_t[x, z * T3 : (z + 1) * T3, :]) for z in range(z0, z0 + 8)], axis=1
            )
            total = total + nt_dot(slab, hid)
        second_ref[rows, :] = total

    for z0 in range(0, QZ, 4):
        acts = jnp.concatenate(
            [
                jnp.concatenate(
                    [act_t[plane, 2 * z * C : (2 * z + 3) * C, :] for z in range(z0, z0 + 4)], axis=1
                )
                for plane in range(IX)
            ],
            axis=0,
        )
        ups = jnp.concatenate(
            [
                jnp.concatenate(
                    [four_blocks(wide[x, z * T3 : (z + 1) * T3, :]) for x in range(QX)], axis=0
                )
                for z in range(z0, z0 + 4)
            ],
            axis=1,
        )
        part = nt_dot(acts, ups)
        if z0 == 0:
            acc[...] = part
        else:
            acc[...] += part
    first_ref[0:T3, :] = acc[T3 : 2 * T3, 128:256]
    first_ref[T3 : 2 * T3, :] = acc[0:T3, 0:128] + acc[2 * T3 : 3 * T3, 128:256]
    first_ref[2 * T3 :, :] = acc[T3 : 2 * T3, 0:128] + acc[3 * T3 :, 128:256]


def last_kernel(grad_next_ref, spread_ref, act_t, first_ref, second_ref, out_ref, wide, flips, dense):
    spread_plane(grad_next_ref, spread_ref, wide)
    total = first_ref[0:T3, :]
    for z0 in range(0, QZ, 4):
        acts = jnp.concatenate(
            [act_t[IX - 1, 2 * z * C : (2 * z + 3) * C, :] for z in range(z0, z0 + 4)], axis=1
        )
        ups = jnp.concatenate(
            [four_blocks(wide[z * T3 : (z + 1) * T3, :]) for z in range(z0, z0 + 4)], axis=1
        )
        total = total + nt_dot(acts, ups)

    turned = jnp.concatenate([total, first_ref[T3:, :]], axis=0).T
    for side in range(3):
        width = min(128, TAPS - side * 128)
        flips[side, 0:128, 0:width] = turned[:, side * 128 : side * 128 + width]
    flips[3] = second_ref[...]
    lane = lax.broadcasted_iota(jnp.int32, (8, 128), 1)
    for ab in range(9):
        ab_rev = (2 - ab // 3) * 3 + (2 - ab % 3)
        for d in range(3):
            for which in range(2):
                row = jnp.zeros((8, 128), F32)
                for r in range(4):
                    if which == 0:
                        side, offset, begin = ab // 4, (ab % 4) * C, d * C + r
                    else:
                        side, offset, begin = 3, d * C, ab_rev * C + r
                    part = flips[side, pl.ds(begin, 8, stride=4), :]
                    turn = (r * C - offset) % 128
                    part = pltpu.roll(part, turn, 1) if turn else part
                    row = jnp.where(lane // C == r, part, row)
                dense[which, (ab * 3 + d) * 8 : (ab * 3 + d + 1) * 8, :] = row

    for s in range(16):
        begin = (27 * s) // 2
        for which in range(2):
            out_ref[s, which, 0:14, :] = dense[which, begin : begin + 14, :]
            out_ref[s, which, 14:16, :] = jnp.zeros((2, 128), F32)


def call(kernel, name, outs, scratch, flops, *args):
    vmem = pl.BlockSpec(memory_space=pltpu.VMEM)
    shapes = [jax.ShapeDtypeStruct(shape, dtype) for shape, dtype in outs]
    moved = sum(a.size * a.dtype.itemsize for a in args)
    return pl.pallas_call(
        kernel,
        out_shape=shapes,
        in_specs=[vmem] * len(args),
        out_specs=[vmem] * len(shapes),
        scratch_shapes=[pltpu.VMEM(shape, dtype) for shape, dtype in scratch],
        compiler_params=pltpu.CompilerParams(vmem_limit_bytes=24 * 2**20),
        cost_estimate=pl.CostEstimate(flops=flops, bytes_accessed=moved, transcendentals=0),
        name=name,
    )(*args)


def relay_cot(cot):
    plane = ((COT_ROWS, QY), BF)
    return call(cot_kernel, "relay_cot", [plane, plane], [((QX, C * QZ, QY), F32)], 10**8, cot)


def local_terms(act, pre, weight, cot0, cot1):
    return call(
        local_kernel,
        "local_terms",
        [
            ((IX, ACT_ROWS, IY), BF),
            ((QX, QZ * T3, QY), BF),
            ((QX, QZ * C, QY), F32),
            ((QX, QZ * C, QY), F32),
            ((2, T3, 128), BF),
            ((QY, 3 * IY), BF),
            ((TAPS, 128), F32),
        ],
        [((2, 2, C * IZ, 128), F32), ((QX, C * QZ, QY), F32), ((3 * 128, 128), F32)],
        5 * 10**9,
        act, pre, weight, cot0, cot1,
    )


def rim_grad(cot_prev, rim_weights, partial, scale):
    return call(
        rim_kernel, "rim_grad", [((QZ * C, QY), BF)], [], 10**9, cot_prev, rim_weights, partial, scale
    )[0]


def main_terms(*args):
    return call(
        main_kernel,
        "main_terms",
        [((TAPS, 128), F32), ((TAPS, 128), F32)],
        [((QZ * C, QY), BF), ((QX, QZ * T3, IY), BF), ((4 * T3, 256), F32)],
        5 * 10**9,
        *args,
    )


def last_terms(*args):
    return call(
        last_kernel,
        "last_terms",
        [((16, 2, 16, 128), F32)],
        [((QZ * T3, IY), BF), ((4, TAPS, 128), F32), ((2, 216, 128), F32)],
        10**9,
        *args,
    )[0]


def moved(x, axis, by):
    length = lax.axis_size(axis)
    pairs = [(i, i + by) for i in range(length) if 0 <= i + by < length]
    return lax.ppermute(x, axis, pairs)


def on_device(activations, preact, cotangent, conv_weight):
    act, pre, cot = activations[0], preact[0], cotangent[0]
    cot0, cot1 = relay_cot(cot)
    cot_prev = moved(cot1, "space", 1)
    cot_next = moved(cot0, "space", -1)
    act_t, hidden_t, scale, partial, rim_weights, spread, second = local_terms(
        act, pre, conv_weight, cot0, cot1
    )
    grad0 = rim_grad(cot_prev, rim_weights, partial, scale)
    grad_next = moved(grad0, "space", -1)
    first, second = main_terms(
        cot_prev, cot_next, rim_weights, partial, scale, hidden_t, act_t, grad0, spread, second
    )
    terms = last_terms(grad_next, spread, act_t, first, second)
    shares = lax.all_to_all(terms.reshape(32, 16, 128), ("space", "lane"), 0, 0, tiled=True)
    share = jnp.sum(shares, axis=0)
    copies = lax.all_to_all(
        jnp.broadcast_to(share[None], (16, 16, 128)), ("deep", "lane"), 0, 0, tiled=True
    )
    total = jnp.sum(copies.reshape(8, 2, 16, 128), axis=0)[:, :14].reshape(2, 14 * 128)
    odd = lax.axis_index("space") % 2
    return lax.dynamic_slice(total, (0, 64 * odd), (2, 1728))


def solution(mesh):
    split = Mesh(mesh.devices.reshape(16, 8, 2), ("space", "deep", "lane"))
    rows = P(("deep", "lane"), None, "space", None, None)
    return jax.shard_map(
        on_device,
        mesh=split,
        in_specs=(rows, rows, rows, P()),
        out_specs=P(None, "space"),
        check_vma=False,
    )
```

```python
import jax
import jax.numpy as jnp
from jax import lax
from jax.experimental import pallas as pl
from jax.experimental.pallas import tpu as pltpu
from jax.sharding import Mesh, PartitionSpec as P

BF = jnp.bfloat16
F32 = jnp.float32

C = 32
QX, QZ, QY = 2, 24, 128
IX, IZ, IY = 4, 48, 256
T3 = 3 * C
COT_ROWS = (QZ + 3) * C
ACT_ROWS = (IZ + 1) * C
TAPS = 9 * C

NT = (((1,), (1,)), ((), ()))


def nt_dot(a, b):
    return lax.dot_general(a, b, NT, preferred_element_type=F32)


def lane_shift(x, by):
    lanes = lax.broadcasted_iota(jnp.int32, x.shape, 1)
    return jnp.where(lanes == (0 if by == 1 else QY - 1), 0.0, pltpu.roll(x, by % QY, 1))


def taps_joined(part):
    return part[C : 2 * C] + lane_shift(part[0:C], -1) + lane_shift(part[2 * C : T3], 1)


def four_blocks(rows):
    return jnp.concatenate([rows, rows[0:C]], axis=0)


def on_odd():
    return lax.rem(lax.axis_index("space"), 2) == 1


def cot_kernel(cot_ref, planes_ref, chip_ref, far_ref, flat):
    odd = on_odd()
    for plane in range(QX):
        planes_ref[plane, 0:C, :] = jnp.zeros((C, QY), BF)
        planes_ref[plane, (QZ + 1) * C :, :] = jnp.zeros((2 * C, QY), BF)
    for plane in range(QX):
        flat[plane] = cot_ref[:, plane].astype(F32).reshape(C * QZ, QY)
        for z in range(QZ):
            block = flat[plane, pl.ds(z, C, stride=QZ), :]
            planes_ref[plane, (z + 1) * C : (z + 2) * C, :] = block.astype(BF)
    chip_ref[...] = jnp.where(odd, planes_ref[0], planes_ref[1])
    far_ref[...] = jnp.where(odd, planes_ref[1], planes_ref[0])


def local_kernel(
    act_ref, pre_ref, weight_ref, planes_ref,
    act_t, hidden_t, scale_t, partial_t, rim_weights, spread_ref, second_ref,
    flat_act, flat_pre, weight_t,
):
    row = lax.broadcasted_iota(jnp.int32, (QY, 3 * IY), 0)
    col = lax.broadcasted_iota(jnp.int32, (QY, 3 * IY), 1)
    spread_ref[...] = jnp.where(col % IY == 2 * row + col // IY - 1, 1.0, 0.0).astype(BF)

    for j in range(3):
        for k in range(3):
            base = (2 - j) * 9 + (2 - k) * 3
            wide = jnp.concatenate([weight_ref[base + d].astype(F32) for d in range(3)], axis=1)
            weight_t[(j * 4 + k) * C : (j * 4 + k + 1) * C, 0:T3] = wide
        weight_t[(j * 4 + 3) * C : (j * 4 + 4) * C, :] = jnp.zeros((C, 128), F32)
    flipped = [weight_t[j * 128 : (j + 1) * 128, 0:T3].T.astype(BF) for j in range(3)]
    rim_weights[0] = flipped[0]
    rim_weights[1] = flipped[2]
    weights = jnp.concatenate(
        [
            jnp.concatenate([flipped[1], flipped[2]], axis=1),
            jnp.concatenate([flipped[0], flipped[1]], axis=1),
        ],
        axis=0,
    )

    for plane in range(QX):
        flat_pre[plane] = pre_ref[:, plane].astype(F32).reshape(C * QZ, QY)
        for z in range(QZ):
            pre = flat_pre[plane, pl.ds(z, C, stride=QZ), :]
            gate = jax.nn.sigmoid(pre)
            hidden = (pre * gate).astype(BF).astype(F32)
            hidden_t[plane, z * T3 : (z + 1) * T3, :] = jnp.concatenate(
                [lane_shift(hidden, 1), hidden, lane_shift(hidden, -1)], axis=0
            ).astype(BF)
            scale_t[plane, z * C : (z + 1) * C, :] = gate * (1.0 + pre * (1.0 - gate))

    for plane in range(IX):
        act_t[plane, 0:C, :] = jnp.zeros((C, IY), BF)
        flat = act_ref[:, plane].astype(F32).reshape(C * IZ, IY)
        for side in range(2):
            flat_act[plane % 2, side] = flat[:, side * 128 : (side + 1) * 128]
        for z in range(IZ):
            for side in range(2):
                tile = flat_act[plane % 2, side, pl.ds(z, C, stride=IZ), :].astype(BF)
                act_t[plane, (z + 1) * C : (z + 2) * C, side * 128 : (side + 1) * 128] = tile

    for z in range(0, QZ, 2):
        slab = jnp.concatenate(
            [
                jnp.concatenate(
                    [planes_ref[x, (z + h) * C : (z + h + 4) * C, :] for h in range(2)], axis=1
                )
                for x in range(QX)
            ],
            axis=0,
        )
        terms = jnp.dot(weights, slab, preferred_element_type=F32)
        for x in range(QX):
            for h in range(2):
                part = terms[x * T3 : (x + 1) * T3, h * QY : (h + 1) * QY]
                partial_t[x, (z + h) * C : (z + h + 1) * C, :] = taps_joined(part)

    total = jnp.zeros((2 * T3, 256), F32)
    for z0 in range(0, QZ, 8):
        slab = jnp.concatenate(
            [
                jnp.concatenate(
                    [planes_ref[x, z * C : (z + 3) * C, :] for z in range(z0, z0 + 8)], axis=1
                )
                for x in range(QX)
            ],
            axis=0,
        )
        hid = jnp.concatenate(
            [
                jnp.concatenate(
                    [four_blocks(hidden_t[x, z * T3 : (z + 1) * T3, :]) for x in range(QX)], axis=0
                )
                for z in range(z0, z0 + 8)
            ],
            axis=1,
        )
        total = total + nt_dot(slab, hid)
    second_ref[0:T3, :] = total[0:T3, 128:256]
    second_ref[T3 : 2 * T3, :] = total[0:T3, 0:128] + total[T3:, 128:256]
    second_ref[2 * T3 :, :] = total[T3:, 0:128]


def pre_grads(cot_ref, weights, partial, scale, put):
    for z in range(0, QZ, 2):
        slab = jnp.concatenate([cot_ref[(z + h) * C : (z + h + 4) * C, :] for h in range(2)], axis=1)
        terms = jnp.dot(weights, slab, preferred_element_type=F32)
        for h in range(2):
            rows = slice((z + h) * C, (z + h + 1) * C)
            grad = partial[rows, :] + taps_joined(terms[:, h * QY : (h + 1) * QY])
            put(rows, (grad * scale[rows, :]).astype(BF))


def rim_kernel(chip_ref, far_ref, rim_weights, partial_ref, scale_ref, out_ref, halo_ref):
    odd = on_odd()
    halo_ref[0] = jnp.where(odd, chip_ref[...], far_ref[...])
    halo_ref[1] = jnp.where(odd, far_ref[...], chip_ref[...])

    def put(rows, value):
        out_ref[rows, :] = value

    pre_grads(halo_ref.at[0], rim_weights[0], partial_ref.at[0], scale_ref.at[0], put)


def spread_plane(grad_ref, spread_ref, wide_ref):
    for z0 in range(0, QZ, 4):
        wide = jnp.dot(
            grad_ref[z0 * C : (z0 + 4) * C, :], spread_ref[...], preferred_element_type=F32
        ).astype(BF)
        for h in range(4):
            for d in range(3):
                begin = (z0 + h) * T3 + d * C
                wide_ref[begin : begin + C, :] = wide[h * C : (h + 1) * C, d * IY : (d + 1) * IY]


def dense_row(flips, second, ab, d):
    lane = lax.broadcasted_iota(jnp.int32, (8, 128), 1)
    row = jnp.zeros((8, 128), F32)
    for r in range(4):
        if second:
            ab_rev = (2 - ab // 3) * 3 + (2 - ab % 3)
            side, offset, begin = 0, d * C, ab_rev * C + r
        else:
            side, offset, begin = ab // 4, (ab % 4) * C, d * C + r
        part = flips[side, pl.ds(begin, 8, stride=4), :]
        turn = (r * C - offset) % 128
        part = pltpu.roll(part, turn, 1) if turn else part
        row = jnp.where(lane // C == r, part, row)
    return row


def main_kernel(
    halo_ref, rim_weights, partial_ref, scale_ref, hidden_t, act_t, grad0_ref,
    spread_ref, second_in,
    first_ref, dense_ref,
    grad1, wide, acc, second_ref, flips,
):
    def put(rows, value):
        grad1[rows, :] = value

    pre_grads(halo_ref.at[1], rim_weights[1], partial_ref.at[1], scale_ref.at[1], put)
    spread_plane(grad0_ref, spread_ref, wide.at[0])
    spread_plane(grad1, spread_ref, wide.at[1])

    second_ref[0, T3 : 2 * T3, :] = second_in[T3 : 2 * T3, :]
    for x in range(QX):
        rows = slice(2 * x * T3, (2 * x + 1) * T3)
        total = second_in[rows, :]
        for z0 in range(0, QZ, 8):
            slab = jnp.concatenate([halo_ref[x, z * C : (z + 3) * C, :] for z in range(z0, z0 + 8)], axis=1)
            hid = jnp.concatenate(
                [four_blocks(hidden_t[x, z * T3 : (z + 1) * T3, :]) for z in range(z0, z0 + 8)], axis=1
            )
            total = total + nt_dot(slab, hid)
        second_ref[0, rows, :] = total
    for ab in range(9):
        for d in range(3):
            begin = (ab * 3 + d) * 8
            dense_ref[1, begin : begin + 8, :] = dense_row(second_ref, True, ab, d)

    for z0 in range(0, QZ, 4):
        acts = jnp.concatenate(
            [
                jnp.concatenate(
                    [act_t[plane, 2 * z * C : (2 * z + 3) * C, :] for z in range(z0, z0 + 4)], axis=1
                )
                for plane in range(IX)
            ],
            axis=0,
        )
        ups = jnp.concatenate(
            [
                jnp.concatenate(
                    [four_blocks(wide[x, z * T3 : (z + 1) * T3, :]) for x in range(QX)], axis=0
                )
                for z in range(z0, z0 + 4)
            ],
            axis=1,
        )
        part = nt_dot(acts, ups)
        if z0 == 0:
            acc[...] = part
        else:
            acc[...] += part
    first_ref[...] = acc[T3 : 2 * T3, 128:256]
    turned = jnp.concatenate(
        [
            acc[0:T3, 0:128] + acc[2 * T3 : 3 * T3, 128:256],
            acc[T3 : 2 * T3, 0:128] + acc[3 * T3 :, 128:256],
        ],
        axis=0,
    ).T
    flips[0] = turned[:, 0:128]
    flips[1, :, 0 : 2 * T3 - 128] = turned[:, 128:]
    for ab in range(6):
        for d in range(3):
            begin = ((ab + 3) * 3 + d) * 8
            dense_ref[0, begin : begin + 8, :] = dense_row(flips, False, ab, d)


def last_kernel(grad_next_ref, spread_ref, act_t, first_ref, dense_ref, out_ref, wide, flips, head):
    spread_plane(grad_next_ref, spread_ref, wide)
    total = first_ref[...]
    for z0 in range(0, QZ, 4):
        acts = jnp.concatenate(
            [act_t[IX - 1, 2 * z * C : (2 * z + 3) * C, :] for z in range(z0, z0 + 4)], axis=1
        )
        ups = jnp.concatenate(
            [four_blocks(wide[z * T3 : (z + 1) * T3, :]) for z in range(z0, z0 + 4)], axis=1
        )
        total = total + nt_dot(acts, ups)

    flips[0, :, 0:T3] = total.T
    for ab in range(3):
        for d in range(3):
            begin = (ab * 3 + d) * 8
            head[begin : begin + 8, :] = dense_row(flips, False, ab, d)

    for s in range(16):
        begin = (27 * s) // 2
        for which in range(2):
            known = min(max(72 - begin, 0), 14) if which == 0 else 0
            if known:
                out_ref[s, which, 0:known, :] = head[begin : begin + known, :]
            if known < 14:
                out_ref[s, which, known:14, :] = dense_ref[which, begin + known : begin + 14, :]
            out_ref[s, which, 14:16, :] = jnp.zeros((2, 128), F32)


VMEM = pltpu.VMEM


def call(kernel, name, outs, scratch, flops, *args):
    shapes = [jax.ShapeDtypeStruct(shape, dtype) for shape, dtype in outs]
    moved = sum(a.size * a.dtype.itemsize for a in args)
    return pl.pallas_call(
        kernel,
        out_shape=shapes,
        in_specs=[pl.BlockSpec(memory_space=VMEM)] * len(args),
        out_specs=[pl.BlockSpec(memory_space=VMEM)] * len(shapes),
        scratch_shapes=scratch,
        compiler_params=pltpu.CompilerParams(vmem_limit_bytes=24 * 2**20),
        cost_estimate=pl.CostEstimate(flops=flops, bytes_accessed=moved, transcendentals=0),
        name=name,
    )(*args)


def relay_cot(cot):
    plane = ((COT_ROWS, QY), BF)
    return call(
        cot_kernel,
        "relay_cot",
        [((QX, COT_ROWS, QY), BF), plane, plane],
        [VMEM((QX, C * QZ, QY), F32)],
        10**10,
        cot,
    )


def local_terms(act, pre, weight, planes):
    return call(
        local_kernel,
        "local_terms",
        [
            ((IX, ACT_ROWS, IY), BF),
            ((QX, QZ * T3, QY), BF),
            ((QX, QZ * C, QY), F32),
            ((QX, QZ * C, QY), F32),
            ((2, T3, 128), BF),
            ((QY, 3 * IY), BF),
            ((TAPS, 128), F32),
        ],
        [
            VMEM((2, 2, C * IZ, 128), F32),
            VMEM((QX, C * QZ, QY), F32),
            VMEM((3 * 128, 128), F32),
        ],
        5 * 10**9,
        act, pre, weight, planes,
    )


def rim_grad(*args):
    return call(
        rim_kernel,
        "rim_grad",
        [((QZ * C, QY), BF), ((QX, COT_ROWS, QY), BF)],
        [],
        10**9,
        *args,
    )


def main_terms(*args):
    return call(
        main_kernel,
        "main_terms",
        [((T3, 128), F32), ((2, 216, 128), F32)],
        [
            VMEM((QZ * C, QY), BF),
            VMEM((QX, QZ * T3, IY), BF),
            VMEM((4 * T3, 256), F32),
            VMEM((1, TAPS, 128), F32),
            VMEM((2, 128, 128), F32),
        ],
        5 * 10**9,
        *args,
    )


def last_terms(*args):
    return call(
        last_kernel,
        "last_terms",
        [((16, 2, 16, 128), F32)],
        [VMEM((QZ * T3, IY), BF), VMEM((1, 128, 128), F32), VMEM((72, 128), F32)],
        10**9,
        *args,
    )[0]


def swapped(x, begin):
    pairs = []
    for i in range(begin, lax.axis_size("space") - 1, 2):
        pairs += [(i, i + 1), (i + 1, i)]
    return lax.ppermute(x, "space", pairs)


def on_device(activations, preact, cotangent, conv_weight):
    act, pre, cot = activations[0], preact[0], cotangent[0]
    planes, to_chip, to_far = relay_cot(cot)
    far = swapped(to_far, 1)
    chip = swapped(to_chip, 0)
    act_t, hidden_t, scale, partial, rim_weights, spread, second = local_terms(
        act, pre, conv_weight, planes
    )
    grad0, halo = rim_grad(chip, far, rim_weights, partial, scale)
    count = lax.axis_size("space")
    grad_next = lax.ppermute(grad0, "space", [(i + 1, i) for i in range(count - 1)])
    first, dense = main_terms(
        halo, rim_weights, partial, scale, hidden_t, act_t, grad0, spread, second
    )
    terms = last_terms(grad_next, spread, act_t, first, dense)
    shares = lax.all_to_all(terms.reshape(32, 16, 128), ("space", "lane"), 0, 0, tiled=True)
    share = jnp.sum(shares, axis=0)
    copies = lax.all_to_all(
        jnp.broadcast_to(share[None], (16, 16, 128)), ("deep", "lane"), 0, 0, tiled=True
    )
    total = jnp.sum(copies.reshape(8, 2, 16, 128), axis=0)[:, :14].reshape(2, 14 * 128)
    odd = lax.axis_index("space") % 2
    return lax.dynamic_slice(total, (0, 64 * odd), (2, 1728))


def solution(mesh):
    split = Mesh(mesh.devices.reshape(16, 8, 2), ("space", "deep", "lane"))
    rows = P(("deep", "lane"), None, "space", None, None)
    return jax.shard_map(
        on_device,
        mesh=split,
        in_specs=(rows, rows, rows, P()),
        out_specs=P(None, "space"),
        check_vma=False,
    )
```

```python
import jax
import jax.numpy as jnp
from jax import lax
from jax.experimental import pallas as pl
from jax.experimental.pallas import tpu as pltpu
from jax.sharding import Mesh, PartitionSpec as P

BF = jnp.bfloat16
F32 = jnp.float32

C = 32
QX, QZ, QY = 2, 24, 128
IX, IZ, IY = 4, 48, 256
T3 = 3 * C
COT_ROWS = (QZ + 3) * C
ACT_ROWS = (IZ + 1) * C
TAPS = 9 * C

NT = (((1,), (1,)), ((), ()))


def nt_dot(a, b):
    return lax.dot_general(a, b, NT, preferred_element_type=F32)


def lane_shift(x, by):
    lanes = lax.broadcasted_iota(jnp.int32, x.shape, 1)
    return jnp.where(lanes == (0 if by == 1 else QY - 1), 0.0, pltpu.roll(x, by % QY, 1))


def taps_joined(part):
    return part[C : 2 * C] + lane_shift(part[0:C], -1) + lane_shift(part[2 * C : T3], 1)


def four_blocks(rows):
    return jnp.concatenate([rows, rows[0:C]], axis=0)


def on_odd():
    return lax.rem(lax.axis_index("space"), 2) == 1


def relay_kernel(cot_ref, planes_ref, chip_ref, far_ref, flat):
    odd = on_odd()
    for plane in range(QX):
        planes_ref[plane, 0:C, :] = jnp.zeros((C, QY), BF)
        planes_ref[plane, (QZ + 1) * C :, :] = jnp.zeros((2 * C, QY), BF)
        flat[plane] = cot_ref[:, plane].astype(F32).reshape(C * QZ, QY)
    for z in range(QZ):
        rows = slice(z * C, (z + 1) * C)
        first, last = [flat[i, pl.ds(z, C, stride=QZ), :].astype(BF) for i in range(QX)]
        planes_ref[0, (z + 1) * C : (z + 2) * C, :] = first
        planes_ref[1, (z + 1) * C : (z + 2) * C, :] = last
        chip_ref[rows, :] = jnp.where(odd, first, last)
        far_ref[rows, :] = jnp.where(odd, last, first)


def prev_kernel(pre_ref, planes_ref, prev_ref, flat):
    flat[...] = pre_ref[:, 0].astype(F32).reshape(C * QZ, QY)
    for z in range(QZ):
        rows = slice(z * C, (z + 1) * C)
        prev_ref[0, rows, :] = flat[pl.ds(z, C, stride=QZ), :].astype(BF)
        prev_ref[1, rows, :] = planes_ref[1, (z + 1) * C : (z + 2) * C, :]


def local_kernel(
    act_ref, pre_ref, weight_ref, planes_ref,
    act_t, hidden_t, scale_t, partial_t, rim_weights, spread_ref, second_ref,
    flat_act, flat_pre, weight_t,
):
    row = lax.broadcasted_iota(jnp.int32, (QY, 3 * IY), 0)
    col = lax.broadcasted_iota(jnp.int32, (QY, 3 * IY), 1)
    spread_ref[...] = jnp.where(col % IY == 2 * row + col // IY - 1, 1.0, 0.0).astype(BF)

    for j in range(3):
        for k in range(3):
            base = (2 - j) * 9 + (2 - k) * 3
            wide = jnp.concatenate([weight_ref[base + d].astype(F32) for d in range(3)], axis=1)
            weight_t[(j * 4 + k) * C : (j * 4 + k + 1) * C, 0:T3] = wide
        weight_t[(j * 4 + 3) * C : (j * 4 + 4) * C, :] = jnp.zeros((C, 128), F32)
    flipped = [weight_t[j * 128 : (j + 1) * 128, 0:T3].T.astype(BF) for j in range(3)]
    for j in range(3):
        rim_weights[j] = flipped[j]
    weights = jnp.concatenate(
        [
            jnp.concatenate([flipped[1], flipped[2]], axis=1),
            jnp.concatenate([flipped[0], flipped[1]], axis=1),
        ],
        axis=0,
    )

    for plane in range(QX):
        flat_pre[plane] = pre_ref[:, plane].astype(F32).reshape(C * QZ, QY)
        for z in range(QZ):
            pre = flat_pre[plane, pl.ds(z, C, stride=QZ), :]
            gate = jax.nn.sigmoid(pre)
            hidden = (pre * gate).astype(BF).astype(F32)
            hidden_t[plane, z * T3 : (z + 1) * T3, :] = jnp.concatenate(
                [lane_shift(hidden, 1), hidden, lane_shift(hidden, -1)], axis=0
            ).astype(BF)
            scale_t[plane, z * C : (z + 1) * C, :] = gate * (1.0 + pre * (1.0 - gate))

    for plane in range(IX):
        act_t[plane, 0:C, :] = jnp.zeros((C, IY), BF)
        flat = act_ref[:, plane].astype(F32).reshape(C * IZ, IY)
        for side in range(2):
            flat_act[plane % 2, side] = flat[:, side * 128 : (side + 1) * 128]
        for z in range(IZ):
            for side in range(2):
                tile = flat_act[plane % 2, side, pl.ds(z, C, stride=IZ), :].astype(BF)
                act_t[plane, (z + 1) * C : (z + 2) * C, side * 128 : (side + 1) * 128] = tile

    for z in range(0, QZ, 2):
        slab = jnp.concatenate(
            [
                jnp.concatenate(
                    [planes_ref[x, (z + h) * C : (z + h + 4) * C, :] for h in range(2)], axis=1
                )
                for x in range(QX)
            ],
            axis=0,
        )
        terms = jnp.dot(weights, slab, preferred_element_type=F32)
        for x in range(QX):
            for h in range(2):
                part = terms[x * T3 : (x + 1) * T3, h * QY : (h + 1) * QY]
                partial_t[x, (z + h) * C : (z + h + 1) * C, :] = taps_joined(part)

    total = jnp.zeros((2 * T3, 256), F32)
    for z0 in range(0, QZ, 8):
        slab = jnp.concatenate(
            [
                jnp.concatenate(
                    [planes_ref[x, z * C : (z + 3) * C, :] for z in range(z0, z0 + 8)], axis=1
                )
                for x in range(QX)
            ],
            axis=0,
        )
        hid = jnp.concatenate(
            [
                jnp.concatenate(
                    [four_blocks(hidden_t[x, z * T3 : (z + 1) * T3, :]) for x in range(QX)], axis=0
                )
                for z in range(z0, z0 + 8)
            ],
            axis=1,
        )
        total = total + nt_dot(slab, hid)
    second_ref[0:T3, :] = total[0:T3, 128:256]
    second_ref[T3 : 2 * T3, :] = total[0:T3, 0:128] + total[T3:, 128:256]
    second_ref[2 * T3 :, :] = total[T3:, 0:128]


def pre_grads(cot_ref, weights, partial, scale, put):
    for z in range(0, QZ, 2):
        slab = jnp.concatenate([cot_ref[(z + h) * C : (z + h + 4) * C, :] for h in range(2)], axis=1)
        terms = jnp.dot(weights, slab, preferred_element_type=F32)
        for h in range(2):
            rows = slice((z + h) * C, (z + h + 1) * C)
            grad = partial[rows, :] + taps_joined(terms[:, h * QY : (h + 1) * QY])
            put(rows, (grad * scale[rows, :]).astype(BF))


def spread_plane(grad_ref, spread_ref, wide_ref):
    for z0 in range(0, QZ, 4):
        wide = jnp.dot(
            grad_ref[z0 * C : (z0 + 4) * C, :], spread_ref[...], preferred_element_type=F32
        ).astype(BF)
        for h in range(4):
            for d in range(3):
                begin = (z0 + h) * T3 + d * C
                wide_ref[begin : begin + C, :] = wide[h * C : (h + 1) * C, d * IY : (d + 1) * IY]


def dense_row(flips, second, ab, d):
    lane = lax.broadcasted_iota(jnp.int32, (8, 128), 1)
    row = jnp.zeros((8, 128), F32)
    for r in range(4):
        if second:
            ab_rev = (2 - ab // 3) * 3 + (2 - ab % 3)
            side, offset, begin = 0, d * C, ab_rev * C + r
        else:
            side, offset, begin = ab // 4, (ab % 4) * C, d * C + r
        part = flips[side, pl.ds(begin, 8, stride=4), :]
        turn = (r * C - offset) % 128
        part = pltpu.roll(part, turn, 1) if turn else part
        row = jnp.where(lane // C == r, part, row)
    return row


def main_kernel(
    chip_ref, far_ref, planes_ref, rim_weights, partial_ref, scale_ref, hidden_t, act_t,
    spread_ref, second_in,
    first_ref, dense_ref, partial_next,
    halo_ref, grads, wide, acc, second_ref, flips,
):
    odd = on_odd()
    for x in range(QX):
        halo_ref[x, 0:C, :] = jnp.zeros((C, QY), BF)
        halo_ref[x, (QZ + 1) * C :, :] = jnp.zeros((2 * C, QY), BF)
    inner = slice(C, (QZ + 1) * C)
    halo_ref[0, inner, :] = jnp.where(odd, chip_ref[...], far_ref[...])
    halo_ref[1, inner, :] = jnp.where(odd, far_ref[...], chip_ref[...])

    for x in range(QX):

        def put(rows, value, x=x):
            grads[x, rows, :] = value

        pre_grads(halo_ref.at[x], rim_weights[2 * x], partial_ref.at[x], scale_ref.at[x], put)
        spread_plane(grads.at[x], spread_ref, wide.at[x])

    second_ref[0, T3 : 2 * T3, :] = second_in[T3 : 2 * T3, :]
    for x in range(QX):
        rows = slice(2 * x * T3, (2 * x + 1) * T3)
        total = second_in[rows, :]
        for z0 in range(0, QZ, 8):
            slab = jnp.concatenate([halo_ref[x, z * C : (z + 3) * C, :] for z in range(z0, z0 + 8)], axis=1)
            hid = jnp.concatenate(
                [four_blocks(hidden_t[x, z * T3 : (z + 1) * T3, :]) for z in range(z0, z0 + 8)], axis=1
            )
            total = total + nt_dot(slab, hid)
        second_ref[0, rows, :] = total
    for ab in range(9):
        for d in range(3):
            begin = (ab * 3 + d) * 8
            dense_ref[1, begin : begin + 8, :] = dense_row(second_ref, True, ab, d)

    for z0 in range(0, QZ, 4):
        acts = jnp.concatenate(
            [
                jnp.concatenate(
                    [act_t[plane, 2 * z * C : (2 * z + 3) * C, :] for z in range(z0, z0 + 4)], axis=1
                )
                for plane in range(IX)
            ],
            axis=0,
        )
        ups = jnp.concatenate(
            [
                jnp.concatenate(
                    [four_blocks(wide[x, z * T3 : (z + 1) * T3, :]) for x in range(QX)], axis=0
                )
                for z in range(z0, z0 + 4)
            ],
            axis=1,
        )
        part = nt_dot(acts, ups)
        if z0 == 0:
            acc[...] = part
        else:
            acc[...] += part
    weights = jnp.concatenate([rim_weights[0], rim_weights[1]], axis=1)
    for z in range(0, QZ, 2):
        slab = jnp.concatenate(
            [
                jnp.concatenate([ref[1, (z + h) * C : (z + h + 4) * C, :] for h in range(2)], axis=1)
                for ref in (planes_ref, halo_ref)
            ],
            axis=0,
        )
        terms = jnp.dot(weights, slab, preferred_element_type=F32)
        for h in range(2):
            partial_next[(z + h) * C : (z + h + 1) * C, :] = taps_joined(
                terms[:, h * QY : (h + 1) * QY]
            )
    first_ref[...] = acc[T3 : 2 * T3, 128:256]
    turned = jnp.concatenate(
        [
            acc[0:T3, 0:128] + acc[2 * T3 : 3 * T3, 128:256],
            acc[T3 : 2 * T3, 0:128] + acc[3 * T3 :, 128:256],
        ],
        axis=0,
    ).T
    flips[0] = turned[:, 0:128]
    flips[1, :, 0 : 2 * T3 - 128] = turned[:, 128:]
    for ab in range(6):
        for d in range(3):
            begin = ((ab + 3) * 3 + d) * 8
            dense_ref[0, begin : begin + 8, :] = dense_row(flips, False, ab, d)


def last_kernel(
    next_ref, rim_weights, partial_ref, spread_ref, act_t, first_ref, dense_ref,
    out_ref,
    plane, scale, grads, wide, flips, head,
):
    more = lax.axis_index("space") < lax.axis_size("space") - 1
    plane[0:C, :] = jnp.zeros((C, QY), BF)
    plane[(QZ + 1) * C :, :] = jnp.zeros((2 * C, QY), BF)
    plane[C : (QZ + 1) * C, :] = next_ref[1]
    pre = next_ref[0].astype(F32)
    gate = jax.nn.sigmoid(pre)
    scale[...] = jnp.where(more, gate * (1.0 + pre * (1.0 - gate)), 0.0)

    def put(rows, value):
        grads[rows, :] = value

    pre_grads(plane, rim_weights[2], partial_ref, scale, put)
    spread_plane(grads, spread_ref, wide)
    total = first_ref[...]
    for z0 in range(0, QZ, 4):
        acts = jnp.concatenate(
            [act_t[IX - 1, 2 * z * C : (2 * z + 3) * C, :] for z in range(z0, z0 + 4)], axis=1
        )
        ups = jnp.concatenate(
            [four_blocks(wide[z * T3 : (z + 1) * T3, :]) for z in range(z0, z0 + 4)], axis=1
        )
        total = total + nt_dot(acts, ups)

    flips[0, :, 0:T3] = total.T
    for ab in range(3):
        for d in range(3):
            begin = (ab * 3 + d) * 8
            head[begin : begin + 8, :] = dense_row(flips, False, ab, d)

    for s in range(16):
        begin = (27 * s) // 2
        for which in range(2):
            known = min(max(72 - begin, 0), 14) if which == 0 else 0
            if known:
                out_ref[s, which, 0:known, :] = head[begin : begin + known, :]
            if known < 14:
                out_ref[s, which, known:14, :] = dense_ref[which, begin + known : begin + 14, :]
            out_ref[s, which, 14:16, :] = jnp.zeros((2, 128), F32)


VMEM = pltpu.VMEM


def call(kernel, name, outs, scratch, flops, *args):
    shapes = [jax.ShapeDtypeStruct(shape, dtype) for shape, dtype in outs]
    moved = sum(a.size * a.dtype.itemsize for a in args)
    return pl.pallas_call(
        kernel,
        out_shape=shapes,
        in_specs=[pl.BlockSpec(memory_space=VMEM)] * len(args),
        out_specs=[pl.BlockSpec(memory_space=VMEM)] * len(shapes),
        scratch_shapes=scratch,
        compiler_params=pltpu.CompilerParams(vmem_limit_bytes=24 * 2**20),
        cost_estimate=pl.CostEstimate(flops=flops, bytes_accessed=moved, transcendentals=0),
        name=name,
    )(*args)


def relay(cot):
    plane = ((QZ * C, QY), BF)
    return call(
        relay_kernel,
        "relay",
        [((QX, COT_ROWS, QY), BF), plane, plane],
        [VMEM((QX, C * QZ, QY), F32)],
        10**10,
        cot,
    )


def for_prev(pre, planes):
    return call(
        prev_kernel, "for_prev", [((2, QZ * C, QY), BF)], [VMEM((C * QZ, QY), F32)], 10**9, pre, planes
    )[0]


def local_terms(act, pre, weight, planes):
    return call(
        local_kernel,
        "local_terms",
        [
            ((IX, ACT_ROWS, IY), BF),
            ((QX, QZ * T3, QY), BF),
            ((QX, QZ * C, QY), F32),
            ((QX, QZ * C, QY), F32),
            ((3, T3, 128), BF),
            ((QY, 3 * IY), BF),
            ((TAPS, 128), F32),
        ],
        [
            VMEM((2, 2, C * IZ, 128), F32),
            VMEM((QX, C * QZ, QY), F32),
            VMEM((3 * 128, 128), F32),
        ],
        5 * 10**9,
        act, pre, weight, planes,
    )


def main_terms(*args):
    return call(
        main_kernel,
        "main_terms",
        [((T3, 128), F32), ((2, 216, 128), F32), ((QZ * C, QY), F32)],
        [
            VMEM((QX, COT_ROWS, QY), BF),
            VMEM((QX, QZ * C, QY), BF),
            VMEM((QX, QZ * T3, IY), BF),
            VMEM((4 * T3, 256), F32),
            VMEM((1, TAPS, 128), F32),
            VMEM((2, 128, 128), F32),
        ],
        5 * 10**9,
        *args,
    )


def last_terms(*args):
    return call(
        last_kernel,
        "last_terms",
        [((16, 2, 16, 128), F32)],
        [
            VMEM((COT_ROWS, QY), BF),
            VMEM((QZ * C, QY), F32),
            VMEM((QZ * C, QY), BF),
            VMEM((QZ * T3, IY), BF),
            VMEM((1, 128, 128), F32),
            VMEM((72, 128), F32),
        ],
        10**9,
        *args,
    )[0]


def swapped(x, begin):
    pairs = []
    for i in range(begin, lax.axis_size("space") - 1, 2):
        pairs += [(i, i + 1), (i + 1, i)]
    return lax.ppermute(x, "space", pairs)


def on_device(activations, preact, cotangent, conv_weight):
    act, pre, cot = activations[0], preact[0], cotangent[0]
    planes, to_chip, to_far = relay(cot)
    to_prev = for_prev(pre, planes)
    far = swapped(to_far, 1)
    after = lax.ppermute(to_prev, "space", [(i + 1, i) for i in range(lax.axis_size("space") - 1)])
    chip = swapped(to_chip, 0)
    act_t, hidden_t, scale, partial, rim_weights, spread, second = local_terms(
        act, pre, conv_weight, planes
    )
    first, dense, partial_next = main_terms(
        chip, far, planes, rim_weights, partial, scale, hidden_t, act_t, spread, second
    )
    terms = last_terms(after, rim_weights, partial_next, spread, act_t, first, dense)
    shares = lax.all_to_all(terms.reshape(32, 16, 128), ("space", "lane"), 0, 0, tiled=True)
    share = jnp.sum(shares, axis=0)
    copies = lax.all_to_all(
        jnp.broadcast_to(share[None], (16, 16, 128)), ("deep", "lane"), 0, 0, tiled=True
    )
    total = jnp.sum(copies.reshape(8, 2, 16, 128), axis=0)[:, :14].reshape(2, 14 * 128)
    odd = lax.axis_index("space") % 2
    return lax.dynamic_slice(total, (0, 64 * odd), (2, 1728))


def solution(mesh):
    split = Mesh(mesh.devices.reshape(16, 8, 2), ("space", "deep", "lane"))
    rows = P(("deep", "lane"), None, "space", None, None)
    return jax.shard_map(
        on_device,
        mesh=split,
        in_specs=(rows, rows, rows, P()),
        out_specs=P(None, "space"),
        check_vma=False,
    )
```

```python
import jax
import jax.numpy as jnp
from jax import lax
from jax.experimental import pallas as pl
from jax.experimental.pallas import tpu as pltpu
from jax.sharding import Mesh, PartitionSpec as P

BF = jnp.bfloat16
F32 = jnp.float32

C = 32
QX, QZ, QY = 2, 24, 128
IX, IZ, IY = 4, 48, 256
T3 = 3 * C
COT_ROWS = (QZ + 3) * C
ACT_ROWS = (IZ + 1) * C
TAPS = 9 * C

NT = (((1,), (1,)), ((), ()))


def nt_dot(a, b):
    return lax.dot_general(a, b, NT, preferred_element_type=F32)


def lane_shift(x, by):
    lanes = lax.broadcasted_iota(jnp.int32, x.shape, 1)
    return jnp.where(lanes == (0 if by == 1 else QY - 1), 0.0, pltpu.roll(x, by % QY, 1))


def by_depth(block):
    channels, depth, last = block.shape
    return jnp.transpose(block, (1, 0, 2)).reshape(depth * channels, last)


def depth_pair(refs, z):
    return jnp.concatenate(
        [
            jnp.concatenate([ref[(z + h) * C : (z + h + 4) * C, :] for h in range(2)], axis=1)
            for ref in refs
        ],
        axis=0,
    )


def taps_joined(part):
    return part[C : 2 * C] + lane_shift(part[0:C], -1) + lane_shift(part[2 * C : T3], 1)


def four_blocks(rows):
    return jnp.concatenate([rows, rows[0:C]], axis=0)


def on_odd():
    return lax.rem(lax.axis_index("space"), 2) == 1


def relay_kernel(cot_ref, planes_ref, chip_ref, far_ref):
    odd = on_odd()
    for plane in range(QX):
        planes_ref[plane, 0:C, :] = jnp.zeros((C, QY), BF)
        planes_ref[plane, (QZ + 1) * C :, :] = jnp.zeros((2 * C, QY), BF)
    first, last = [by_depth(cot_ref[:, plane]) for plane in range(QX)]
    planes_ref[0, C : (QZ + 1) * C, :] = first
    planes_ref[1, C : (QZ + 1) * C, :] = last
    chip_ref[...] = jnp.where(odd, first, last)
    far_ref[...] = jnp.where(odd, last, first)


def prev_kernel(pre_ref, planes_ref, prev_ref):
    prev_ref[0] = by_depth(pre_ref[:, 0])
    prev_ref[1] = planes_ref[1, C : (QZ + 1) * C, :]


def hidden_rows(hidden_t, z0):
    return jnp.concatenate(
        [
            jnp.concatenate(
                [four_blocks(hidden_t[x, z * T3 : (z + 1) * T3, :]) for x in range(QX)], axis=0
            )
            for z in range(z0, z0 + 8)
        ],
        axis=1,
    )


def weight_rows(blocks):
    return jnp.concatenate([jnp.concatenate(row, axis=1) for row in blocks], axis=0)


def local_kernel(
    act_ref, pre_ref, weight_ref, planes_ref,
    act_t, hidden_t, scale_t, partial_t, rim_weights, spread_ref, second_ref,
    weight_t,
):
    row = lax.broadcasted_iota(jnp.int32, (QY, 3 * IY), 0)
    col = lax.broadcasted_iota(jnp.int32, (QY, 3 * IY), 1)
    spread_ref[...] = jnp.where(col % IY == 2 * row + col // IY - 1, 1.0, 0.0).astype(BF)

    for j in range(3):
        for k in range(3):
            base = (2 - j) * 9 + (2 - k) * 3
            wide = jnp.concatenate([weight_ref[base + d].astype(F32) for d in range(3)], axis=1)
            weight_t[(j * 4 + k) * C : (j * 4 + k + 1) * C, 0:T3] = wide
        weight_t[(j * 4 + 3) * C : (j * 4 + 4) * C, :] = jnp.zeros((C, 128), F32)
    flipped = [weight_t[j * 128 : (j + 1) * 128, 0:T3].T.astype(BF) for j in range(3)]
    none = jnp.zeros((T3, 128), BF)
    weights = weight_rows(((flipped[1], flipped[2]), (flipped[0], flipped[1]), (none, flipped[0])))
    rim_weights[...] = weight_rows(((flipped[0], none), (none, flipped[2]), (none, flipped[1])))

    for plane in range(QX):
        rows = by_depth(pre_ref[:, plane]).astype(F32)
        for z in range(QZ):
            pre = rows[z * C : (z + 1) * C]
            gate = jax.nn.sigmoid(pre)
            hidden = (pre * gate).astype(BF).astype(F32)
            hidden_t[plane, z * T3 : (z + 1) * T3, :] = jnp.concatenate(
                [lane_shift(hidden, 1), hidden, lane_shift(hidden, -1)], axis=0
            ).astype(BF)
            scale_t[plane, z * C : (z + 1) * C, :] = gate * (1.0 + pre * (1.0 - gate))

    for plane in range(IX):
        act_t[plane, 0:C, :] = jnp.zeros((C, IY), BF)
        act_t[plane, C:, :] = by_depth(act_ref[:, plane])

    for z in range(0, QZ, 2):
        slab = depth_pair([planes_ref.at[x] for x in range(QX)], z)
        terms = jnp.dot(weights, slab, preferred_element_type=F32)
        for x in range(QX + 1):
            for h in range(2):
                part = terms[x * T3 : (x + 1) * T3, h * QY : (h + 1) * QY]
                partial_t[x, (z + h) * C : (z + h + 1) * C, :] = taps_joined(part)

    total = jnp.zeros((2 * T3, 256), F32)
    for z0 in range(0, QZ, 8):
        slab = jnp.concatenate(
            [
                jnp.concatenate(
                    [planes_ref[x, z * C : (z + 3) * C, :] for z in range(z0, z0 + 8)], axis=1
                )
                for x in range(QX)
            ],
            axis=0,
        )
        total = total + nt_dot(slab, hidden_rows(hidden_t, z0))
    second_ref[0:T3, :] = total[0:T3, 128:256]
    second_ref[T3 : 2 * T3, :] = total[0:T3, 0:128] + total[T3:, 128:256]
    second_ref[2 * T3 :, :] = total[T3:, 0:128]


def spread_plane(grad_ref, spread_ref, wide_ref):
    for z0 in range(0, QZ, 4):
        wide = jnp.dot(
            grad_ref[z0 * C : (z0 + 4) * C, :], spread_ref[...], preferred_element_type=F32
        ).astype(BF)
        for h in range(4):
            for d in range(3):
                begin = (z0 + h) * T3 + d * C
                wide_ref[begin : begin + C, :] = wide[h * C : (h + 1) * C, d * IY : (d + 1) * IY]


def dense_row(flips, second, ab, d):
    lane = lax.broadcasted_iota(jnp.int32, (8, 128), 1)
    row = jnp.zeros((8, 128), F32)
    for r in range(4):
        if second:
            ab_rev = (2 - ab // 3) * 3 + (2 - ab % 3)
            side, offset, begin = 0, d * C, ab_rev * C + r
        else:
            side, offset, begin = ab // 4, (ab % 4) * C, d * C + r
        part = flips[side, pl.ds(begin, 8, stride=4), :]
        turn = (r * C - offset) % 128
        part = pltpu.roll(part, turn, 1) if turn else part
        row = jnp.where(lane // C == r, part, row)
    return row


def main_kernel(
    far_ref, chip_ref, rim_weights, partial_ref, scale_ref, hidden_t, act_t,
    spread_ref, second_in,
    first_ref, dense_ref, partial_next,
    halo_ref, grads, wide, acc, second_ref, flips,
):
    odd = on_odd()
    for x in range(QX):
        halo_ref[x, 0:C, :] = jnp.zeros((C, QY), BF)
        halo_ref[x, (QZ + 1) * C :, :] = jnp.zeros((2 * C, QY), BF)
    inner = slice(C, (QZ + 1) * C)
    halo_ref[0, inner, :] = jnp.where(odd, chip_ref[...], far_ref[...])
    halo_ref[1, inner, :] = jnp.where(odd, far_ref[...], chip_ref[...])

    for z in range(0, QZ, 2):
        slab = depth_pair([halo_ref.at[x] for x in range(QX)], z)
        terms = jnp.dot(rim_weights[...], slab, preferred_element_type=F32)
        for h in range(2):
            rows = slice((z + h) * C, (z + h + 1) * C)
            parts = [
                partial_ref[x, rows, :]
                + taps_joined(terms[x * T3 : (x + 1) * T3, h * QY : (h + 1) * QY])
                for x in range(QX + 1)
            ]
            for x in range(QX):
                grads[x, rows, :] = (parts[x] * scale_ref[x, rows, :]).astype(BF)
            partial_next[rows, :] = parts[QX]
    for x in range(QX):
        spread_plane(grads.at[x], spread_ref, wide.at[x])

    total = jnp.zeros((2 * T3, 256), F32)
    for z0 in range(0, QZ, 8):
        slab = jnp.concatenate(
            [
                jnp.concatenate([halo_ref[x, z * C : (z + 3) * C, :] for z in range(z0, z0 + 8)], axis=1)
                for x in range(QX)
            ],
            axis=0,
        )
        total = total + nt_dot(slab, hidden_rows(hidden_t, z0))
    second_ref[0, 0:T3, :] = second_in[0:T3, :] + total[0:T3, 0:128]
    second_ref[0, T3 : 2 * T3, :] = second_in[T3 : 2 * T3, :]
    second_ref[0, 2 * T3 :, :] = second_in[2 * T3 :, :] + total[T3:, 128:256]
    for ab in range(9):
        for d in range(3):
            begin = (ab * 3 + d) * 8
            dense_ref[1, begin : begin + 8, :] = dense_row(second_ref, True, ab, d)

    for z0 in range(0, QZ, 4):
        acts = jnp.concatenate(
            [
                jnp.concatenate(
                    [act_t[plane, 2 * z * C : (2 * z + 3) * C, :] for z in range(z0, z0 + 4)], axis=1
                )
                for plane in range(IX)
            ],
            axis=0,
        )
        ups = jnp.concatenate(
            [
                jnp.concatenate(
                    [four_blocks(wide[x, z * T3 : (z + 1) * T3, :]) for x in range(QX)], axis=0
                )
                for z in range(z0, z0 + 4)
            ],
            axis=1,
        )
        part = nt_dot(acts, ups)
        if z0 == 0:
            acc[...] = part
        else:
            acc[...] += part
    first_ref[...] = acc[T3 : 2 * T3, 128:256]
    turned = jnp.concatenate(
        [
            acc[0:T3, 0:128] + acc[2 * T3 : 3 * T3, 128:256],
            acc[T3 : 2 * T3, 0:128] + acc[3 * T3 :, 128:256],
        ],
        axis=0,
    ).T
    flips[0] = turned[:, 0:128]
    flips[1, :, 0 : 2 * T3 - 128] = turned[:, 128:]
    for ab in range(6):
        for d in range(3):
            begin = ((ab + 3) * 3 + d) * 8
            dense_ref[0, begin : begin + 8, :] = dense_row(flips, False, ab, d)


def last_kernel(
    next_ref, rim_weights, partial_ref, spread_ref, act_t, first_ref, dense_ref,
    out_ref,
    plane, scale, grads, wide, flips, head,
):
    more = lax.axis_index("space") < lax.axis_size("space") - 1
    plane[0:C, :] = jnp.zeros((C, QY), BF)
    plane[(QZ + 1) * C :, :] = jnp.zeros((2 * C, QY), BF)
    plane[C : (QZ + 1) * C, :] = next_ref[1]
    pre = next_ref[0].astype(F32)
    gate = jax.nn.sigmoid(pre)
    scale[...] = jnp.where(more, gate * (1.0 + pre * (1.0 - gate)), 0.0)

    weights = rim_weights[T3 : 2 * T3, 128:256]
    for z in range(0, QZ, 2):
        terms = jnp.dot(weights, depth_pair([plane], z), preferred_element_type=F32)
        for h in range(2):
            rows = slice((z + h) * C, (z + h + 1) * C)
            grad = partial_ref[rows, :] + taps_joined(terms[:, h * QY : (h + 1) * QY])
            grads[rows, :] = (grad * scale[rows, :]).astype(BF)
    spread_plane(grads, spread_ref, wide)
    total = first_ref[...]
    for z0 in range(0, QZ, 4):
        acts = jnp.concatenate(
            [act_t[IX - 1, 2 * z * C : (2 * z + 3) * C, :] for z in range(z0, z0 + 4)], axis=1
        )
        ups = jnp.concatenate(
            [four_blocks(wide[z * T3 : (z + 1) * T3, :]) for z in range(z0, z0 + 4)], axis=1
        )
        total = total + nt_dot(acts, ups)

    flips[0, :, 0:T3] = total.T
    for ab in range(3):
        for d in range(3):
            begin = (ab * 3 + d) * 8
            head[begin : begin + 8, :] = dense_row(flips, False, ab, d)

    for s in range(16):
        begin = (27 * s) // 2
        for which in range(2):
            known = min(max(72 - begin, 0), 14) if which == 0 else 0
            if known:
                out_ref[s, which, 0:known, :] = head[begin : begin + known, :]
            if known < 14:
                out_ref[s, which, known:14, :] = dense_ref[which, begin + known : begin + 14, :]
            out_ref[s, which, 14:16, :] = jnp.zeros((2, 128), F32)


def share_kernel(shares_ref, copies_ref):
    total = shares_ref[0].astype(F32)
    for i in range(1, 32):
        total = total + shares_ref[i].astype(F32)
    for i in range(16):
        copies_ref[i] = total.astype(copies_ref.dtype)


def total_kernel(copies_ref, out_ref):
    odd = on_odd()
    lane = lax.broadcasted_iota(jnp.int32, (16, 128), 1)
    rows = []
    for which in range(2):
        total = copies_ref[which].astype(F32)
        for deep in range(1, 8):
            total = total + copies_ref[2 * deep + which].astype(F32)
        turned = pltpu.roll(total, 64, 1)
        after = jnp.concatenate([turned[1:], turned[0:1]], axis=0)
        rows.append(jnp.where(odd, jnp.where(lane < 64, turned, after), total))
    for k in range(14):
        width = min(128, 1728 - 128 * k)
        both = jnp.concatenate([rows[0][k : k + 1], rows[1][k : k + 1]], axis=0)
        out_ref[:, 128 * k : 128 * k + width] = both[:, 0:width]


VMEM = pltpu.VMEM


def call(kernel, name, outs, scratch, flops, *args):
    shapes = [jax.ShapeDtypeStruct(shape, dtype) for shape, dtype in outs]
    moved = sum(a.size * a.dtype.itemsize for a in args)
    return pl.pallas_call(
        kernel,
        out_shape=shapes,
        in_specs=[pl.BlockSpec(memory_space=VMEM)] * len(args),
        out_specs=[pl.BlockSpec(memory_space=VMEM)] * len(shapes),
        scratch_shapes=scratch,
        compiler_params=pltpu.CompilerParams(vmem_limit_bytes=24 * 2**20),
        cost_estimate=pl.CostEstimate(flops=flops, bytes_accessed=moved, transcendentals=0),
        name=name,
    )(*args)


def relay(cot):
    plane = ((QZ * C, QY), BF)
    return call(
        relay_kernel,
        "relay",
        [((QX, COT_ROWS, QY), BF), plane, plane],
        [],
        10**10,
        cot,
    )


def for_prev(pre, planes):
    return call(
        prev_kernel, "for_prev", [((2, QZ * C, QY), BF)], [], 10**9, pre, planes
    )[0]


def local_terms(act, pre, weight, planes):
    return call(
        local_kernel,
        "local_terms",
        [
            ((IX, ACT_ROWS, IY), BF),
            ((QX, QZ * T3, QY), BF),
            ((QX, QZ * C, QY), F32),
            ((QX + 1, QZ * C, QY), F32),
            ((3 * T3, 256), BF),
            ((QY, 3 * IY), BF),
            ((TAPS, 128), F32),
        ],
        [
            VMEM((3 * 128, 128), F32),
        ],
        5 * 10**9,
        act, pre, weight, planes,
    )


def main_terms(*args):
    return call(
        main_kernel,
        "main_terms",
        [((T3, 128), F32), ((2, 216, 128), F32), ((QZ * C, QY), F32)],
        [
            VMEM((QX, COT_ROWS, QY), BF),
            VMEM((QX, QZ * C, QY), BF),
            VMEM((QX, QZ * T3, IY), BF),
            VMEM((4 * T3, 256), F32),
            VMEM((1, TAPS, 128), F32),
            VMEM((2, 128, 128), F32),
        ],
        5 * 10**9,
        *args,
    )


def last_terms(*args):
    return call(
        last_kernel,
        "last_terms",
        [((16, 2, 16, 128), F32)],
        [
            VMEM((COT_ROWS, QY), BF),
            VMEM((QZ * C, QY), F32),
            VMEM((QZ * C, QY), BF),
            VMEM((QZ * T3, IY), BF),
            VMEM((1, 128, 128), F32),
            VMEM((72, 128), F32),
        ],
        10**9,
        *args,
    )[0]


def share_copies(shares):
    return call(share_kernel, "share_copies", [((16, 16, 128), F32)], [], 10**6, shares)[0]


def total_rows(copies):
    return call(total_kernel, "total_rows", [((2, 1728), F32)], [], 10**6, copies)[0]


def swapped(x, begin):
    pairs = []
    for i in range(begin, lax.axis_size("space") - 1, 2):
        pairs += [(i, i + 1), (i + 1, i)]
    return lax.ppermute(x, "space", pairs)


def on_device(activations, preact, cotangent, conv_weight):
    act, pre, cot = activations[0], preact[0], cotangent[0]
    planes, to_chip, to_far = relay(cot)
    to_prev = for_prev(pre, planes)
    far = swapped(to_far, 1)
    after = lax.ppermute(to_prev, "space", [(i + 1, i) for i in range(lax.axis_size("space") - 1)])
    chip = swapped(to_chip, 0)
    act_t, hidden_t, scale, partial, rim_weights, spread, second = local_terms(
        act, pre, conv_weight, planes
    )
    first, dense, partial_next = main_terms(
        far, chip, rim_weights, partial, scale, hidden_t, act_t, spread, second
    )
    terms = last_terms(after, rim_weights, partial_next, spread, act_t, first, dense)
    shares = lax.all_to_all(terms.reshape(32, 16, 128), ("space", "lane"), 0, 0, tiled=True)
    copies = lax.all_to_all(share_copies(shares), ("deep", "lane"), 0, 0, tiled=True)
    return total_rows(copies)


def solution(mesh):
    split = Mesh(mesh.devices.reshape(16, 8, 2), ("space", "deep", "lane"))
    rows = P(("deep", "lane"), None, "space", None, None)
    return jax.shard_map(
        on_device,
        mesh=split,
        in_specs=(rows, rows, rows, P()),
        out_specs=P(None, "space"),
        check_vma=False,
    )
```

```python
import jax
import jax.numpy as jnp
from jax import lax
from jax.experimental import pallas as pl
from jax.experimental.pallas import tpu as pltpu
from jax.sharding import Mesh, PartitionSpec as P

BF = jnp.bfloat16
F32 = jnp.float32

C = 32
QX, QZ, QY = 2, 24, 128
IX, IZ, IY = 4, 48, 256
T3 = 3 * C
COT_ROWS = (QZ + 3) * C
ACT_ROWS = (IZ + 1) * C
TAPS = 9 * C

NT = (((1,), (1,)), ((), ()))


def nt_dot(a, b):
    return lax.dot_general(a, b, NT, preferred_element_type=F32)


def lane_shift(x, by):
    lanes = lax.broadcasted_iota(jnp.int32, x.shape, 1)
    return jnp.where(lanes == (0 if by == 1 else QY - 1), 0.0, pltpu.roll(x, by % QY, 1))


def by_depth(block):
    channels, depth, last = block.shape
    return jnp.transpose(block, (1, 0, 2)).reshape(depth * channels, last)


def depth_pair(refs, z):
    return jnp.concatenate(
        [
            jnp.concatenate([ref[(z + h) * C : (z + h + 4) * C, :] for h in range(2)], axis=1)
            for ref in refs
        ],
        axis=0,
    )


def taps_joined(part):
    return part[C : 2 * C] + lane_shift(part[0:C], -1) + lane_shift(part[2 * C : T3], 1)


def four_blocks(rows):
    return jnp.concatenate([rows, rows[0:C]], axis=0)


def on_odd():
    return lax.rem(lax.axis_index("space"), 2) == 1


def relay_kernel(cot_ref, planes_ref, chip_ref, far_ref):
    odd = on_odd()
    for plane in range(QX):
        planes_ref[plane, 0:C, :] = jnp.zeros((C, QY), BF)
        planes_ref[plane, (QZ + 1) * C :, :] = jnp.zeros((2 * C, QY), BF)
    first, last = [by_depth(cot_ref[:, plane]) for plane in range(QX)]
    planes_ref[0, C : (QZ + 1) * C, :] = first
    planes_ref[1, C : (QZ + 1) * C, :] = last
    chip_ref[...] = jnp.where(odd, first, last)
    far_ref[...] = jnp.where(odd, last, first)


def prev_kernel(pre_ref, planes_ref, prev_ref):
    prev_ref[0] = by_depth(pre_ref[:, 0])
    prev_ref[1] = planes_ref[1, C : (QZ + 1) * C, :]


def hidden_rows(hidden_t, z0):
    return jnp.concatenate(
        [
            jnp.concatenate(
                [four_blocks(hidden_t[x, z * T3 : (z + 1) * T3, :]) for x in range(QX)], axis=0
            )
            for z in range(z0, z0 + 8)
        ],
        axis=1,
    )


def weight_rows(blocks):
    return jnp.concatenate([jnp.concatenate(row, axis=1) for row in blocks], axis=0)


def local_kernel(
    act_ref, pre_ref, weight_ref, planes_ref,
    act_t, hidden_t, scale_t, partial_t, rim_weights, spread_ref, second_ref,
    weight_t,
):
    row = lax.broadcasted_iota(jnp.int32, (QY, 3 * IY), 0)
    col = lax.broadcasted_iota(jnp.int32, (QY, 3 * IY), 1)
    spread_ref[...] = jnp.where(col % IY == 2 * row + col // IY - 1, 1.0, 0.0).astype(BF)

    for j in range(3):
        for k in range(3):
            base = (2 - j) * 9 + (2 - k) * 3
            wide = jnp.concatenate([weight_ref[base + d].astype(F32) for d in range(3)], axis=1)
            weight_t[(j * 4 + k) * C : (j * 4 + k + 1) * C, 0:T3] = wide
        weight_t[(j * 4 + 3) * C : (j * 4 + 4) * C, :] = jnp.zeros((C, 128), F32)
    flipped = [weight_t[j * 128 : (j + 1) * 128, 0:T3].T.astype(BF) for j in range(3)]
    none = jnp.zeros((T3, 128), BF)
    weights = weight_rows(((flipped[1], flipped[2]), (flipped[0], flipped[1]), (none, flipped[0])))
    rim_weights[...] = weight_rows(((flipped[0], none), (none, flipped[2]), (none, flipped[1])))

    for plane in range(QX):
        rows = by_depth(pre_ref[:, plane]).astype(F32)
        for z in range(QZ):
            pre = rows[z * C : (z + 1) * C]
            gate = jax.nn.sigmoid(pre)
            hidden = (pre * gate).astype(BF).astype(F32)
            hidden_t[plane, z * T3 : (z + 1) * T3, :] = jnp.concatenate(
                [lane_shift(hidden, 1), hidden, lane_shift(hidden, -1)], axis=0
            ).astype(BF)
            scale_t[plane, z * C : (z + 1) * C, :] = gate * (1.0 + pre * (1.0 - gate))

    for plane in range(IX):
        act_t[plane, 0:C, :] = jnp.zeros((C, IY), BF)
        act_t[plane, C:, :] = by_depth(act_ref[:, plane])

    for z in range(0, QZ, 2):
        slab = depth_pair([planes_ref.at[x] for x in range(QX)], z)
        terms = jnp.dot(weights, slab, preferred_element_type=F32)
        for x in range(QX + 1):
            for h in range(2):
                part = terms[x * T3 : (x + 1) * T3, h * QY : (h + 1) * QY]
                partial_t[x, (z + h) * C : (z + h + 1) * C, :] = taps_joined(part)

    total = jnp.zeros((2 * T3, 256), F32)
    for z0 in range(0, QZ, 8):
        slab = jnp.concatenate(
            [
                jnp.concatenate(
                    [planes_ref[x, z * C : (z + 3) * C, :] for z in range(z0, z0 + 8)], axis=1
                )
                for x in range(QX)
            ],
            axis=0,
        )
        total = total + nt_dot(slab, hidden_rows(hidden_t, z0))
    second_ref[0:T3, :] = total[0:T3, 128:256]
    second_ref[T3 : 2 * T3, :] = total[0:T3, 0:128] + total[T3:, 128:256]
    second_ref[2 * T3 :, :] = total[T3:, 0:128]


def spread_plane(grad_ref, spread_ref, wide_ref):
    for z0 in range(0, QZ, 4):
        wide = jnp.dot(
            grad_ref[z0 * C : (z0 + 4) * C, :], spread_ref[...], preferred_element_type=F32
        ).astype(BF)
        for h in range(4):
            for d in range(3):
                begin = (z0 + h) * T3 + d * C
                wide_ref[begin : begin + C, :] = wide[h * C : (h + 1) * C, d * IY : (d + 1) * IY]


def dense_row(flips, second, ab, d):
    lane = lax.broadcasted_iota(jnp.int32, (8, 128), 1)
    row = jnp.zeros((8, 128), F32)
    for r in range(4):
        if second:
            ab_rev = (2 - ab // 3) * 3 + (2 - ab % 3)
            side, offset, begin = 0, d * C, ab_rev * C + r
        else:
            side, offset, begin = ab // 4, (ab % 4) * C, d * C + r
        part = flips[side, pl.ds(begin, 8, stride=4), :]
        turn = (r * C - offset) % 128
        part = pltpu.roll(part, turn, 1) if turn else part
        row = jnp.where(lane // C == r, part, row)
    return row


def main_kernel(
    far_ref, chip_ref, rim_weights, partial_ref, scale_ref, hidden_t, act_t,
    spread_ref, second_in,
    first_ref, dense_ref, partial_next,
    halo_ref, grads, wide, acc, second_ref, flips,
):
    odd = on_odd()
    for x in range(QX):
        halo_ref[x, 0:C, :] = jnp.zeros((C, QY), BF)
        halo_ref[x, (QZ + 1) * C :, :] = jnp.zeros((2 * C, QY), BF)
    inner = slice(C, (QZ + 1) * C)
    halo_ref[0, inner, :] = jnp.where(odd, chip_ref[...], far_ref[...])
    halo_ref[1, inner, :] = jnp.where(odd, far_ref[...], chip_ref[...])

    for z in range(0, QZ, 2):
        slab = depth_pair([halo_ref.at[x] for x in range(QX)], z)
        terms = jnp.dot(rim_weights[...], slab, preferred_element_type=F32)
        for h in range(2):
            rows = slice((z + h) * C, (z + h + 1) * C)
            parts = [
                partial_ref[x, rows, :]
                + taps_joined(terms[x * T3 : (x + 1) * T3, h * QY : (h + 1) * QY])
                for x in range(QX + 1)
            ]
            for x in range(QX):
                grads[x, rows, :] = (parts[x] * scale_ref[x, rows, :]).astype(BF)
            partial_next[rows, :] = parts[QX]
    for x in range(QX):
        spread_plane(grads.at[x], spread_ref, wide.at[x])

    total = jnp.zeros((2 * T3, 256), F32)
    for z0 in range(0, QZ, 8):
        slab = jnp.concatenate(
            [
                jnp.concatenate([halo_ref[x, z * C : (z + 3) * C, :] for z in range(z0, z0 + 8)], axis=1)
                for x in range(QX)
            ],
            axis=0,
        )
        total = total + nt_dot(slab, hidden_rows(hidden_t, z0))
    second_ref[0, 0:T3, :] = second_in[0:T3, :] + total[0:T3, 0:128]
    second_ref[0, T3 : 2 * T3, :] = second_in[T3 : 2 * T3, :]
    second_ref[0, 2 * T3 :, :] = second_in[2 * T3 :, :] + total[T3:, 128:256]
    for ab in range(9):
        for d in range(3):
            begin = (ab * 3 + d) * 8
            dense_ref[1, begin : begin + 8, :] = dense_row(second_ref, True, ab, d)

    for z0 in range(0, QZ, 4):
        acts = jnp.concatenate(
            [
                jnp.concatenate(
                    [act_t[plane, 2 * z * C : (2 * z + 3) * C, :] for z in range(z0, z0 + 4)], axis=1
                )
                for plane in range(IX)
            ],
            axis=0,
        )
        ups = jnp.concatenate(
            [
                jnp.concatenate(
                    [four_blocks(wide[x, z * T3 : (z + 1) * T3, :]) for x in range(QX)], axis=0
                )
                for z in range(z0, z0 + 4)
            ],
            axis=1,
        )
        part = nt_dot(acts, ups)
        if z0 == 0:
            acc[...] = part
        else:
            acc[...] += part
    first_ref[...] = acc[T3 : 2 * T3, 128:256]
    turned = jnp.concatenate(
        [
            acc[0:T3, 0:128] + acc[2 * T3 : 3 * T3, 128:256],
            acc[T3 : 2 * T3, 0:128] + acc[3 * T3 :, 128:256],
        ],
        axis=0,
    ).T
    flips[0] = turned[:, 0:128]
    flips[1, :, 0 : 2 * T3 - 128] = turned[:, 128:]
    for ab in range(6):
        for d in range(3):
            begin = ((ab + 3) * 3 + d) * 8
            dense_ref[0, begin : begin + 8, :] = dense_row(flips, False, ab, d)


def last_kernel(
    next_ref, rim_weights, partial_ref, spread_ref, act_t, first_ref, dense_ref,
    out_ref,
    plane, scale, grads, wide, flips, head,
):
    more = lax.axis_index("space") < lax.axis_size("space") - 1
    plane[0:C, :] = jnp.zeros((C, QY), BF)
    plane[(QZ + 1) * C :, :] = jnp.zeros((2 * C, QY), BF)
    plane[C : (QZ + 1) * C, :] = next_ref[1]
    pre = next_ref[0].astype(F32)
    gate = jax.nn.sigmoid(pre)
    scale[...] = jnp.where(more, gate * (1.0 + pre * (1.0 - gate)), 0.0)

    weights = rim_weights[T3 : 2 * T3, 128:256]
    for z in range(0, QZ, 2):
        terms = jnp.dot(weights, depth_pair([plane], z), preferred_element_type=F32)
        for h in range(2):
            rows = slice((z + h) * C, (z + h + 1) * C)
            grad = partial_ref[rows, :] + taps_joined(terms[:, h * QY : (h + 1) * QY])
            grads[rows, :] = (grad * scale[rows, :]).astype(BF)
    spread_plane(grads, spread_ref, wide)
    total = first_ref[...]
    for z0 in range(0, QZ, 4):
        acts = jnp.concatenate(
            [act_t[IX - 1, 2 * z * C : (2 * z + 3) * C, :] for z in range(z0, z0 + 4)], axis=1
        )
        ups = jnp.concatenate(
            [four_blocks(wide[z * T3 : (z + 1) * T3, :]) for z in range(z0, z0 + 4)], axis=1
        )
        total = total + nt_dot(acts, ups)

    flips[0, :, 0:T3] = total.T
    for ab in range(3):
        for d in range(3):
            begin = (ab * 3 + d) * 8
            head[begin : begin + 8, :] = dense_row(flips, False, ab, d)

    for s in range(16):
        begin = (27 * s) // 2
        for which in range(2):
            known = min(max(72 - begin, 0), 14) if which == 0 else 0
            begins = [head[begin : begin + known, :]] if known else []
            if known < 14:
                begins.append(dense_ref[which, begin + known : begin + 14, :])
            begins.append(jnp.zeros((2, 128), F32))
            out_ref[s, which] = jnp.concatenate(begins, axis=0).astype(BF)


def share_kernel(shares_ref, copies_ref):
    total = shares_ref[0].astype(F32)
    for i in range(1, 32):
        total = total + shares_ref[i].astype(F32)
    for i in range(16):
        copies_ref[i] = total.astype(copies_ref.dtype)


def total_kernel(copies_ref, out_ref):
    odd = on_odd()
    lane = lax.broadcasted_iota(jnp.int32, (16, 128), 1)
    rows = []
    for which in range(2):
        total = copies_ref[which].astype(F32)
        for deep in range(1, 8):
            total = total + copies_ref[2 * deep + which].astype(F32)
        turned = pltpu.roll(total, 64, 1)
        after = jnp.concatenate([turned[1:], turned[0:1]], axis=0)
        rows.append(jnp.where(odd, jnp.where(lane < 64, turned, after), total))
    for k in range(14):
        width = min(128, 1728 - 128 * k)
        both = jnp.concatenate([rows[0][k : k + 1], rows[1][k : k + 1]], axis=0)
        out_ref[:, 128 * k : 128 * k + width] = both[:, 0:width]


VMEM = pltpu.VMEM


def call(kernel, name, outs, scratch, flops, *args):
    shapes = [jax.ShapeDtypeStruct(shape, dtype) for shape, dtype in outs]
    moved = sum(a.size * a.dtype.itemsize for a in args)
    return pl.pallas_call(
        kernel,
        out_shape=shapes,
        in_specs=[pl.BlockSpec(memory_space=VMEM)] * len(args),
        out_specs=[pl.BlockSpec(memory_space=VMEM)] * len(shapes),
        scratch_shapes=scratch,
        compiler_params=pltpu.CompilerParams(vmem_limit_bytes=24 * 2**20),
        cost_estimate=pl.CostEstimate(flops=flops, bytes_accessed=moved, transcendentals=0),
        name=name,
    )(*args)


def relay(cot):
    plane = ((QZ * C, QY), BF)
    return call(
        relay_kernel,
        "relay",
        [((QX, COT_ROWS, QY), BF), plane, plane],
        [],
        10**10,
        cot,
    )


def for_prev(pre, planes):
    return call(
        prev_kernel, "for_prev", [((2, QZ * C, QY), BF)], [], 10**9, pre, planes
    )[0]


def local_terms(act, pre, weight, planes):
    return call(
        local_kernel,
        "local_terms",
        [
            ((IX, ACT_ROWS, IY), BF),
            ((QX, QZ * T3, QY), BF),
            ((QX, QZ * C, QY), F32),
            ((QX + 1, QZ * C, QY), F32),
            ((3 * T3, 256), BF),
            ((QY, 3 * IY), BF),
            ((TAPS, 128), F32),
        ],
        [
            VMEM((3 * 128, 128), F32),
        ],
        5 * 10**9,
        act, pre, weight, planes,
    )


def main_terms(*args):
    return call(
        main_kernel,
        "main_terms",
        [((T3, 128), F32), ((2, 216, 128), F32), ((QZ * C, QY), F32)],
        [
            VMEM((QX, COT_ROWS, QY), BF),
            VMEM((QX, QZ * C, QY), BF),
            VMEM((QX, QZ * T3, IY), BF),
            VMEM((4 * T3, 256), F32),
            VMEM((1, TAPS, 128), F32),
            VMEM((2, 128, 128), F32),
        ],
        5 * 10**9,
        *args,
    )


def last_terms(*args):
    return call(
        last_kernel,
        "last_terms",
        [((16, 2, 16, 128), BF)],
        [
            VMEM((COT_ROWS, QY), BF),
            VMEM((QZ * C, QY), F32),
            VMEM((QZ * C, QY), BF),
            VMEM((QZ * T3, IY), BF),
            VMEM((1, 128, 128), F32),
            VMEM((72, 128), F32),
        ],
        10**9,
        *args,
    )[0]


def share_copies(shares):
    return call(share_kernel, "share_copies", [((16, 16, 128), BF)], [], 10**6, shares)[0]


def total_rows(copies):
    return call(total_kernel, "total_rows", [((2, 1728), F32)], [], 10**6, copies)[0]


def swapped(x, begin):
    pairs = []
    for i in range(begin, lax.axis_size("space") - 1, 2):
        pairs += [(i, i + 1), (i + 1, i)]
    return lax.ppermute(x, "space", pairs)


def on_device(activations, preact, cotangent, conv_weight):
    act, pre, cot = activations[0], preact[0], cotangent[0]
    planes, to_chip, to_far = relay(cot)
    to_prev = for_prev(pre, planes)
    far = swapped(to_far, 1)
    after = lax.ppermute(to_prev, "space", [(i + 1, i) for i in range(lax.axis_size("space") - 1)])
    chip = swapped(to_chip, 0)
    act_t, hidden_t, scale, partial, rim_weights, spread, second = local_terms(
        act, pre, conv_weight, planes
    )
    first, dense, partial_next = main_terms(
        far, chip, rim_weights, partial, scale, hidden_t, act_t, spread, second
    )
    terms = last_terms(after, rim_weights, partial_next, spread, act_t, first, dense)
    shares = lax.all_to_all(terms.reshape(32, 16, 128), ("space", "lane"), 0, 0, tiled=True)
    copies = lax.all_to_all(share_copies(shares), ("deep", "lane"), 0, 0, tiled=True)
    return total_rows(copies)


def solution(mesh):
    split = Mesh(mesh.devices.reshape(16, 8, 2), ("space", "deep", "lane"))
    rows = P(("deep", "lane"), None, "space", None, None)
    return jax.shard_map(
        on_device,
        mesh=split,
        in_specs=(rows, rows, rows, P()),
        out_specs=P(None, "space"),
        check_vma=False,
    )
```

```python
import jax
import jax.numpy as jnp
from jax import lax
from jax.experimental import pallas as pl
from jax.experimental.pallas import tpu as pltpu
from jax.sharding import Mesh, PartitionSpec as P

BF = jnp.bfloat16
F32 = jnp.float32

C = 32
QX, QZ, QY = 2, 24, 128
IX, IZ, IY = 4, 48, 256
T3 = 3 * C
COT_ROWS = (QZ + 3) * C
ACT_ROWS = (IZ + 1) * C
TAPS = 9 * C

NT = (((1,), (1,)), ((), ()))


def nt_dot(a, b):
    return lax.dot_general(a, b, NT, preferred_element_type=F32)


def lane_shift(x, by):
    lanes = lax.broadcasted_iota(jnp.int32, x.shape, 1)
    return jnp.where(lanes == (0 if by == 1 else QY - 1), 0.0, pltpu.roll(x, by % QY, 1))


def by_depth(block):
    channels, depth, last = block.shape
    return jnp.transpose(block, (1, 0, 2)).reshape(depth * channels, last)


def depth_pair(refs, z):
    return jnp.concatenate(
        [
            jnp.concatenate([ref[(z + h) * C : (z + h + 4) * C, :] for h in range(2)], axis=1)
            for ref in refs
        ],
        axis=0,
    )


def taps_joined(part):
    return part[C : 2 * C] + lane_shift(part[0:C], -1) + lane_shift(part[2 * C : T3], 1)


def four_blocks(rows):
    return jnp.concatenate([rows, rows[0:C]], axis=0)


def on_odd():
    return lax.rem(lax.axis_index("space"), 2) == 1


def relay_kernel(cot_ref, planes_ref, chip_ref, far_ref):
    odd = on_odd()
    for plane in range(QX):
        planes_ref[plane, 0:C, :] = jnp.zeros((C, QY), BF)
        planes_ref[plane, (QZ + 1) * C :, :] = jnp.zeros((2 * C, QY), BF)
    first, last = [by_depth(cot_ref[:, plane]) for plane in range(QX)]
    planes_ref[0, C : (QZ + 1) * C, :] = first
    planes_ref[1, C : (QZ + 1) * C, :] = last
    chip_ref[...] = jnp.where(odd, first, last)
    far_ref[...] = jnp.where(odd, last, first)


def prev_kernel(pre_ref, planes_ref, prev_ref):
    prev_ref[0] = by_depth(pre_ref[:, 0])
    prev_ref[1] = planes_ref[1, C : (QZ + 1) * C, :]


def hidden_rows(hidden_t, z0):
    return jnp.concatenate(
        [
            jnp.concatenate(
                [four_blocks(hidden_t[x, z * T3 : (z + 1) * T3, :]) for x in range(QX)], axis=0
            )
            for z in range(z0, z0 + 8)
        ],
        axis=1,
    )


def weight_rows(blocks):
    return jnp.concatenate([jnp.concatenate(row, axis=1) for row in blocks], axis=0)


def local_kernel(
    act_ref, pre_ref, weight_ref, planes_ref,
    act_t, hidden_t, scale_t, partial_t, rim_weights, second_ref,
    weight_t,
):
    for j in range(3):
        for k in range(3):
            base = (2 - j) * 9 + (2 - k) * 3
            wide = jnp.concatenate([weight_ref[base + d].astype(F32) for d in range(3)], axis=1)
            weight_t[(j * 4 + k) * C : (j * 4 + k + 1) * C, 0:T3] = wide
        weight_t[(j * 4 + 3) * C : (j * 4 + 4) * C, :] = jnp.zeros((C, 128), F32)
    flipped = [weight_t[j * 128 : (j + 1) * 128, 0:T3].T.astype(BF) for j in range(3)]
    none = jnp.zeros((T3, 128), BF)
    weights = weight_rows(((flipped[1], flipped[2]), (flipped[0], flipped[1]), (none, flipped[0])))
    rim_weights[...] = weight_rows(((flipped[0], none), (none, flipped[2]), (none, flipped[1])))

    for plane in range(QX):
        rows = by_depth(pre_ref[:, plane]).astype(F32)
        for z in range(QZ):
            pre = rows[z * C : (z + 1) * C]
            gate = jax.nn.sigmoid(pre)
            hidden = (pre * gate).astype(BF).astype(F32)
            hidden_t[plane, z * T3 : (z + 1) * T3, :] = jnp.concatenate(
                [lane_shift(hidden, 1), hidden, lane_shift(hidden, -1)], axis=0
            ).astype(BF)
            scale_t[plane, z * C : (z + 1) * C, :] = gate * (1.0 + pre * (1.0 - gate))

    row = lax.broadcasted_iota(jnp.int32, (IY, IY), 0)
    col = lax.broadcasted_iota(jnp.int32, (IY, IY), 1)
    split = jnp.where(row == 2 * (col % QY) + col // QY, 1.0, 0.0).astype(BF)
    for plane in range(IX):
        act_t[plane, 0:C, :] = jnp.zeros((C, IY), BF)
        rows = act_ref[:, plane].reshape(C * IZ, IY)
        rows = jnp.dot(rows, split, preferred_element_type=F32).astype(BF)
        act_t[plane, C:, :] = by_depth(rows.reshape(C, IZ, IY))

    for z in range(0, QZ, 2):
        slab = depth_pair([planes_ref.at[x] for x in range(QX)], z)
        terms = jnp.dot(weights, slab, preferred_element_type=F32)
        for x in range(QX + 1):
            for h in range(2):
                part = terms[x * T3 : (x + 1) * T3, h * QY : (h + 1) * QY]
                partial_t[x, (z + h) * C : (z + h + 1) * C, :] = taps_joined(part)

    total = jnp.zeros((2 * T3, 256), F32)
    for z0 in range(0, QZ, 8):
        slab = jnp.concatenate(
            [
                jnp.concatenate(
                    [planes_ref[x, z * C : (z + 3) * C, :] for z in range(z0, z0 + 8)], axis=1
                )
                for x in range(QX)
            ],
            axis=0,
        )
        total = total + nt_dot(slab, hidden_rows(hidden_t, z0))
    second_ref[0:T3, :] = total[0:T3, 128:256]
    second_ref[T3 : 2 * T3, :] = total[0:T3, 0:128] + total[T3:, 128:256]
    second_ref[2 * T3 :, :] = total[T3:, 0:128]


def put_grad(even_ref, odd_ref, z, grad):
    here = grad.astype(BF)
    even_ref[z * C : (z + 1) * C, :] = here
    odd_ref[2 * z * C : (2 * z + 1) * C, :] = lane_shift(grad, -1).astype(BF)
    odd_ref[(2 * z + 1) * C : (2 * z + 2) * C, :] = here


def cell_sums(act_t, planes, even_refs, odd_refs):
    totals = [0.0, 0.0]
    for z0 in range(0, QZ, 8):
        for side, (refs, step) in enumerate(((even_refs, C), (odd_refs, 2 * C))):
            lanes = slice(side * QY, (side + 1) * QY)
            acts = jnp.concatenate(
                [
                    jnp.concatenate(
                        [act_t[plane, 2 * z * C : (2 * z + 3) * C, lanes] for z in range(z0, z0 + 8)],
                        axis=1,
                    )
                    for plane in planes
                ],
                axis=0,
            )
            grads = jnp.concatenate(
                [
                    jnp.concatenate([ref[z * step : (z + 1) * step, :] for z in range(z0, z0 + 8)], axis=1)
                    for ref in refs
                ],
                axis=0,
            )
            totals[side] = totals[side] + nt_dot(acts, grads)
    return totals


def dense_row(blocks):
    lane = lax.broadcasted_iota(jnp.int32, (8, 128), 1)
    row = jnp.zeros((8, 128), F32)
    for r, (source, begin, offset) in enumerate(blocks):
        part = source[pl.ds(begin, 8, stride=4), :]
        turn = (r * C - offset) % 128
        part = pltpu.roll(part, turn, 1) if turn else part
        row = jnp.where(lane // C == r, part, row)
    return row


def second_row(source, ab, d):
    ab_rev = (2 - ab // 3) * 3 + (2 - ab % 3)
    return dense_row([(source, ab_rev * C + r, d * C) for r in range(4)])


def first_row(flips, ab, d):
    begin = (C, 0, 2 * C)[d]
    return dense_row([(flips.at[ab // 4], begin + r, (ab % 4) * C) for r in range(4)])


def first_flips(flips, side, total):
    rows = slice(0, C) if side == 0 else slice(C, T3)
    turned = total.T
    for begin in range(0, total.shape[0], 128):
        width = min(128, total.shape[0] - begin)
        flips[begin // 128, rows, 0:width] = turned[:, begin : begin + width]


def main_kernel(
    far_ref, chip_ref, rim_weights, partial_ref, scale_ref, hidden_t, act_t,
    second_in,
    first_ref, dense_ref, partial_next,
    halo_ref, even, odds, second_ref, flips,
):
    odd = on_odd()
    for x in range(QX):
        halo_ref[x, 0:C, :] = jnp.zeros((C, QY), BF)
        halo_ref[x, (QZ + 1) * C :, :] = jnp.zeros((2 * C, QY), BF)
    inner = slice(C, (QZ + 1) * C)
    halo_ref[0, inner, :] = jnp.where(odd, chip_ref[...], far_ref[...])
    halo_ref[1, inner, :] = jnp.where(odd, far_ref[...], chip_ref[...])

    for z in range(0, QZ, 2):
        slab = depth_pair([halo_ref.at[x] for x in range(QX)], z)
        terms = jnp.dot(rim_weights[...], slab, preferred_element_type=F32)
        for h in range(2):
            rows = slice((z + h) * C, (z + h + 1) * C)
            parts = [
                partial_ref[x, rows, :]
                + taps_joined(terms[x * T3 : (x + 1) * T3, h * QY : (h + 1) * QY])
                for x in range(QX + 1)
            ]
            for x in range(QX):
                put_grad(even.at[x], odds.at[x], z + h, parts[x] * scale_ref[x, rows, :])
            partial_next[rows, :] = parts[QX]

    total = jnp.zeros((2 * T3, 256), F32)
    for z0 in range(0, QZ, 8):
        slab = jnp.concatenate(
            [
                jnp.concatenate([halo_ref[x, z * C : (z + 3) * C, :] for z in range(z0, z0 + 8)], axis=1)
                for x in range(QX)
            ],
            axis=0,
        )
        total = total + nt_dot(slab, hidden_rows(hidden_t, z0))
    second_ref[0:T3, :] = second_in[0:T3, :] + total[0:T3, 0:128]
    second_ref[T3 : 2 * T3, :] = second_in[T3 : 2 * T3, :]
    second_ref[2 * T3 :, :] = second_in[2 * T3 :, :] + total[T3:, 128:256]
    for ab in range(9):
        for d in range(3):
            begin = (ab * 3 + d) * 8
            dense_ref[1, begin : begin + 8, :] = second_row(second_ref, ab, d)

    even_sum, odd_sum = cell_sums(
        act_t, range(IX), [even.at[x] for x in range(QX)], [odds.at[x] for x in range(QX)]
    )
    even_sum, odd_sum = [
        [total[plane * T3 : (plane + 1) * T3] for plane in range(IX)] for total in (even_sum, odd_sum)
    ]
    first_ref[0, :, 0:C] = even_sum[1][:, C : 2 * C]
    first_ref[1, :, 0 : 2 * C] = odd_sum[1][:, 2 * C :]
    for side, (total, width) in enumerate(((even_sum, C), (odd_sum, 2 * C))):
        joined = jnp.concatenate(
            [total[p][:, 0:width] + total[p + 2][:, width : 2 * width] for p in range(2)], axis=0
        )
        first_flips(flips, side, joined)
    for ab in range(6):
        for d in range(3):
            begin = ((ab + 3) * 3 + d) * 8
            dense_ref[0, begin : begin + 8, :] = first_row(flips, ab, d)


def last_kernel(
    next_ref, rim_weights, partial_ref, act_t, first_ref, dense_ref,
    out_ref,
    plane, scale, even, odds, flips, head,
):
    more = lax.axis_index("space") < lax.axis_size("space") - 1
    plane[0:C, :] = jnp.zeros((C, QY), BF)
    plane[(QZ + 1) * C :, :] = jnp.zeros((2 * C, QY), BF)
    plane[C : (QZ + 1) * C, :] = next_ref[1]
    pre = next_ref[0].astype(F32)
    gate = jax.nn.sigmoid(pre)
    scale[...] = jnp.where(more, gate * (1.0 + pre * (1.0 - gate)), 0.0)

    weights = rim_weights[T3 : 2 * T3, 128:256]
    for z in range(0, QZ, 2):
        terms = jnp.dot(weights, depth_pair([plane], z), preferred_element_type=F32)
        for h in range(2):
            rows = slice((z + h) * C, (z + h + 1) * C)
            grad = partial_ref[rows, :] + taps_joined(terms[:, h * QY : (h + 1) * QY])
            put_grad(even, odds, z + h, grad * scale[rows, :])
    even_sum, odd_sum = cell_sums(act_t, [IX - 1], [even], [odds])
    first_flips(flips, 0, even_sum + first_ref[0, :, 0:C])
    first_flips(flips, 1, odd_sum + first_ref[1, :, 0 : 2 * C])
    for ab in range(3):
        for d in range(3):
            begin = (ab * 3 + d) * 8
            head[begin : begin + 8, :] = first_row(flips, ab, d)

    for s in range(16):
        begin = (27 * s) // 2
        for which in range(2):
            known = min(max(72 - begin, 0), 14) if which == 0 else 0
            begins = [head[begin : begin + known, :]] if known else []
            if known < 14:
                begins.append(dense_ref[which, begin + known : begin + 14, :])
            begins.append(jnp.zeros((2, 128), F32))
            out_ref[s, which] = jnp.concatenate(begins, axis=0).astype(BF)


def share_kernel(shares_ref, copies_ref):
    total = shares_ref[0].astype(F32)
    for i in range(1, 32):
        total = total + shares_ref[i].astype(F32)
    for i in range(16):
        copies_ref[i] = total.astype(copies_ref.dtype)


def total_kernel(copies_ref, out_ref):
    odd = on_odd()
    lane = lax.broadcasted_iota(jnp.int32, (16, 128), 1)
    rows = []
    for which in range(2):
        total = copies_ref[8 * which].astype(F32)
        for deep in range(1, 8):
            total = total + copies_ref[8 * which + deep].astype(F32)
        turned = pltpu.roll(total, 64, 1)
        after = jnp.concatenate([turned[1:], turned[0:1]], axis=0)
        rows.append(jnp.where(odd, jnp.where(lane < 64, turned, after), total))
    for k in range(14):
        width = min(128, 1728 - 128 * k)
        both = jnp.concatenate([rows[0][k : k + 1], rows[1][k : k + 1]], axis=0)
        out_ref[:, 128 * k : 128 * k + width] = both[:, 0:width]


VMEM = pltpu.VMEM


def call(kernel, name, outs, scratch, flops, *args):
    shapes = [jax.ShapeDtypeStruct(shape, dtype) for shape, dtype in outs]
    moved = sum(a.size * a.dtype.itemsize for a in args)
    return pl.pallas_call(
        kernel,
        out_shape=shapes,
        in_specs=[pl.BlockSpec(memory_space=VMEM)] * len(args),
        out_specs=[pl.BlockSpec(memory_space=VMEM)] * len(shapes),
        scratch_shapes=scratch,
        compiler_params=pltpu.CompilerParams(vmem_limit_bytes=24 * 2**20),
        cost_estimate=pl.CostEstimate(flops=flops, bytes_accessed=moved, transcendentals=0),
        name=name,
    )(*args)


def relay(cot):
    plane = ((QZ * C, QY), BF)
    return call(
        relay_kernel,
        "relay",
        [((QX, COT_ROWS, QY), BF), plane, plane],
        [],
        10**10,
        cot,
    )


def for_prev(pre, planes):
    return call(
        prev_kernel, "for_prev", [((2, QZ * C, QY), BF)], [], 10**9, pre, planes
    )[0]


def local_terms(act, pre, weight, planes):
    return call(
        local_kernel,
        "local_terms",
        [
            ((IX, ACT_ROWS, IY), BF),
            ((QX, QZ * T3, QY), BF),
            ((QX, QZ * C, QY), F32),
            ((QX + 1, QZ * C, QY), F32),
            ((3 * T3, 256), BF),
            ((TAPS, 128), F32),
        ],
        [
            VMEM((3 * 128, 128), F32),
        ],
        5 * 10**9,
        act, pre, weight, planes,
    )


def main_terms(*args):
    return call(
        main_kernel,
        "main_terms",
        [((2, T3, 128), F32), ((2, 216, 128), F32), ((QZ * C, QY), F32)],
        [
            VMEM((QX, COT_ROWS, QY), BF),
            VMEM((QX, QZ * C, QY), BF),
            VMEM((QX, QZ * 2 * C, QY), BF),
            VMEM((TAPS, 128), F32),
            VMEM((2, T3, 128), F32),
        ],
        5 * 10**9,
        *args,
    )


def last_terms(*args):
    return call(
        last_kernel,
        "last_terms",
        [((16, 2, 16, 128), BF)],
        [
            VMEM((COT_ROWS, QY), BF),
            VMEM((QZ * C, QY), F32),
            VMEM((QZ * C, QY), BF),
            VMEM((QZ * 2 * C, QY), BF),
            VMEM((1, T3, 128), F32),
            VMEM((72, 128), F32),
        ],
        10**9,
        *args,
    )[0]


def share_copies(shares):
    return call(share_kernel, "share_copies", [((16, 16, 128), BF)], [], 10**6, shares)[0]


def total_rows(copies):
    return call(total_kernel, "total_rows", [((2, 1728), F32)], [], 10**6, copies)[0]


def swapped(x, begin):
    pairs = []
    for i in range(begin, lax.axis_size("space") - 1, 2):
        pairs += [(i, i + 1), (i + 1, i)]
    return lax.ppermute(x, "space", pairs)


def on_device(activations, preact, cotangent, conv_weight):
    act, pre, cot = activations[0], preact[0], cotangent[0]
    planes, to_chip, to_far = relay(cot)
    to_prev = for_prev(pre, planes)
    far = swapped(to_far, 1)
    after = lax.ppermute(to_prev, "space", [(i + 1, i) for i in range(lax.axis_size("space") - 1)])
    chip = swapped(to_chip, 0)
    act_t, hidden_t, scale, partial, rim_weights, second = local_terms(
        act, pre, conv_weight, planes
    )
    first, dense, partial_next = main_terms(
        far, chip, rim_weights, partial, scale, hidden_t, act_t, second
    )
    terms = last_terms(after, rim_weights, partial_next, act_t, first, dense)
    shares = lax.all_to_all(terms.reshape(32, 16, 128), ("space", "lane"), 0, 0, tiled=True)
    copies = lax.all_to_all(share_copies(shares), ("lane", "deep"), 0, 0, tiled=True)
    return total_rows(copies)


def solution(mesh):
    split = Mesh(mesh.devices.reshape(16, 8, 2), ("space", "deep", "lane"))
    rows = P(("deep", "lane"), None, "space", None, None)
    return jax.shard_map(
        on_device,
        mesh=split,
        in_specs=(rows, rows, rows, P()),
        out_specs=P(None, "space"),
        check_vma=False,
    )
```

```python
import jax
import jax.numpy as jnp
from jax import lax
from jax.experimental import pallas as pl
from jax.experimental.pallas import tpu as pltpu
from jax.sharding import Mesh, PartitionSpec as P

BF = jnp.bfloat16
F32 = jnp.float32

C = 32
QX, QZ, QY = 2, 24, 128
IX, IZ, IY = 4, 48, 256
T3 = 3 * C
COT_ROWS = (QZ + 3) * C
ACT_ROWS = (IZ + 1) * C
TAPS = 9 * C

NT = (((1,), (1,)), ((), ()))

SHARE_ORDER = [divmod((i + 22) % 32, 2) for i in range(32)]
COPY_ORDER = [(lane, (i + 4) % 8) for lane in (1, 0) for i in range(8)]


def nt_dot(a, b):
    return lax.dot_general(a, b, NT, preferred_element_type=F32)


def lane_shift(x, by):
    lanes = lax.broadcasted_iota(jnp.int32, x.shape, 1)
    return jnp.where(lanes == (0 if by == 1 else QY - 1), 0.0, pltpu.roll(x, by % QY, 1))


def by_depth(block):
    channels, depth, last = block.shape
    return jnp.transpose(block, (1, 0, 2)).reshape(depth * channels, last)


def depth_pair(refs, z):
    return jnp.concatenate(
        [
            jnp.concatenate([ref[(z + h) * C : (z + h + 4) * C, :] for h in range(2)], axis=1)
            for ref in refs
        ],
        axis=0,
    )


def taps_joined(part):
    return part[C : 2 * C] + lane_shift(part[0:C], -1) + lane_shift(part[2 * C : T3], 1)


def four_blocks(rows):
    return jnp.concatenate([rows, rows[0:C]], axis=0)


def on_odd():
    return lax.rem(lax.axis_index("space"), 2) == 1


def relay_kernel(cot_ref, planes_ref, chip_ref, far_ref):
    odd = on_odd()
    for plane in range(QX):
        planes_ref[plane, 0:C, :] = jnp.zeros((C, QY), BF)
        planes_ref[plane, (QZ + 1) * C :, :] = jnp.zeros((2 * C, QY), BF)
    first, last = [by_depth(cot_ref[:, plane]) for plane in range(QX)]
    planes_ref[0, C : (QZ + 1) * C, :] = first
    planes_ref[1, C : (QZ + 1) * C, :] = last
    chip_ref[...] = jnp.where(odd, first, last)
    far_ref[...] = jnp.where(odd, last, first)


def prev_kernel(pre_ref, planes_ref, prev_ref):
    prev_ref[0] = by_depth(pre_ref[:, 0])
    prev_ref[1] = planes_ref[1, C : (QZ + 1) * C, :]


def hidden_rows(hidden_t, z0):
    return jnp.concatenate(
        [
            jnp.concatenate(
                [four_blocks(hidden_t[x, z * T3 : (z + 1) * T3, :]) for x in range(QX)], axis=0
            )
            for z in range(z0, z0 + 8)
        ],
        axis=1,
    )


def weight_rows(blocks):
    return jnp.concatenate([jnp.concatenate(row, axis=1) for row in blocks], axis=0)


def local_kernel(
    act_ref, pre_ref, weight_ref, planes_ref,
    act_t, hidden_t, scale_t, partial_t, rim_weights, second_ref,
    weight_t,
):
    for j in range(3):
        for k in range(3):
            base = (2 - j) * 9 + (2 - k) * 3
            wide = jnp.concatenate([weight_ref[base + d].astype(F32) for d in range(3)], axis=1)
            weight_t[(j * 4 + k) * C : (j * 4 + k + 1) * C, 0:T3] = wide
        weight_t[(j * 4 + 3) * C : (j * 4 + 4) * C, :] = jnp.zeros((C, 128), F32)
    flipped = [weight_t[j * 128 : (j + 1) * 128, 0:T3].T.astype(BF) for j in range(3)]
    none = jnp.zeros((T3, 128), BF)
    weights = weight_rows(((flipped[1], flipped[2]), (flipped[0], flipped[1]), (none, flipped[0])))
    rim_weights[...] = weight_rows(((flipped[0], none), (none, flipped[2]), (none, flipped[1])))

    for plane in range(QX):
        rows = by_depth(pre_ref[:, plane]).astype(F32)
        for z in range(QZ):
            pre = rows[z * C : (z + 1) * C]
            gate = jax.nn.sigmoid(pre)
            hidden = (pre * gate).astype(BF).astype(F32)
            hidden_t[plane, z * T3 : (z + 1) * T3, :] = jnp.concatenate(
                [lane_shift(hidden, 1), hidden, lane_shift(hidden, -1)], axis=0
            ).astype(BF)
            scale_t[plane, z * C : (z + 1) * C, :] = gate * (1.0 + pre * (1.0 - gate))

    row = lax.broadcasted_iota(jnp.int32, (IY, IY), 0)
    col = lax.broadcasted_iota(jnp.int32, (IY, IY), 1)
    split = jnp.where(row == 2 * (col % QY) + col // QY, 1.0, 0.0).astype(BF)
    for plane in range(IX):
        act_t[plane, 0:C, :] = jnp.zeros((C, IY), BF)
        rows = act_ref[:, plane].reshape(C * IZ, IY)
        rows = jnp.dot(rows, split, preferred_element_type=F32).astype(BF)
        act_t[plane, C:, :] = by_depth(rows.reshape(C, IZ, IY))

    for z in range(0, QZ, 2):
        slab = depth_pair([planes_ref.at[x] for x in range(QX)], z)
        terms = jnp.dot(weights, slab, preferred_element_type=F32)
        for x in range(QX + 1):
            for h in range(2):
                part = terms[x * T3 : (x + 1) * T3, h * QY : (h + 1) * QY]
                partial_t[x, (z + h) * C : (z + h + 1) * C, :] = taps_joined(part)

    total = jnp.zeros((2 * T3, 256), F32)
    for z0 in range(0, QZ, 8):
        slab = jnp.concatenate(
            [
                jnp.concatenate(
                    [planes_ref[x, z * C : (z + 3) * C, :] for z in range(z0, z0 + 8)], axis=1
                )
                for x in range(QX)
            ],
            axis=0,
        )
        total = total + nt_dot(slab, hidden_rows(hidden_t, z0))
    second_ref[0:T3, :] = total[0:T3, 128:256]
    second_ref[T3 : 2 * T3, :] = total[0:T3, 0:128] + total[T3:, 128:256]
    second_ref[2 * T3 :, :] = total[T3:, 0:128]


def put_grad(even_ref, odd_ref, z, grad):
    here = grad.astype(BF)
    even_ref[z * C : (z + 1) * C, :] = here
    odd_ref[2 * z * C : (2 * z + 1) * C, :] = lane_shift(grad, -1).astype(BF)
    odd_ref[(2 * z + 1) * C : (2 * z + 2) * C, :] = here


def cell_sums(act_t, planes, even_refs, odd_refs):
    totals = [0.0, 0.0]
    for z0 in range(0, QZ, 8):
        for side, (refs, step) in enumerate(((even_refs, C), (odd_refs, 2 * C))):
            lanes = slice(side * QY, (side + 1) * QY)
            acts = jnp.concatenate(
                [
                    jnp.concatenate(
                        [act_t[plane, 2 * z * C : (2 * z + 3) * C, lanes] for z in range(z0, z0 + 8)],
                        axis=1,
                    )
                    for plane in planes
                ],
                axis=0,
            )
            grads = jnp.concatenate(
                [
                    jnp.concatenate([ref[z * step : (z + 1) * step, :] for z in range(z0, z0 + 8)], axis=1)
                    for ref in refs
                ],
                axis=0,
            )
            totals[side] = totals[side] + nt_dot(acts, grads)
    return totals


def dense_row(blocks):
    lane = lax.broadcasted_iota(jnp.int32, (8, 128), 1)
    row = jnp.zeros((8, 128), F32)
    for r, (source, begin, offset) in enumerate(blocks):
        part = source[pl.ds(begin, 8, stride=4), :]
        turn = (r * C - offset) % 128
        part = pltpu.roll(part, turn, 1) if turn else part
        row = jnp.where(lane // C == r, part, row)
    return row


def second_row(source, ab, d):
    ab_rev = (2 - ab // 3) * 3 + (2 - ab % 3)
    return dense_row([(source, ab_rev * C + r, d * C) for r in range(4)])


def first_row(flips, ab, d):
    begin = (C, 0, 2 * C)[d]
    return dense_row([(flips.at[ab // 4], begin + r, (ab % 4) * C) for r in range(4)])


def first_flips(flips, side, total):
    rows = slice(0, C) if side == 0 else slice(C, T3)
    turned = total.T
    for begin in range(0, total.shape[0], 128):
        width = min(128, total.shape[0] - begin)
        flips[begin // 128, rows, 0:width] = turned[:, begin : begin + width]


def main_kernel(
    far_ref, chip_ref, rim_weights, partial_ref, scale_ref, hidden_t, act_t,
    second_in,
    first_ref, dense_ref, partial_next,
    halo_ref, even, odds, second_ref, flips,
):
    odd = on_odd()
    for x in range(QX):
        halo_ref[x, 0:C, :] = jnp.zeros((C, QY), BF)
        halo_ref[x, (QZ + 1) * C :, :] = jnp.zeros((2 * C, QY), BF)
    inner = slice(C, (QZ + 1) * C)
    halo_ref[0, inner, :] = jnp.where(odd, chip_ref[...], far_ref[...])
    halo_ref[1, inner, :] = jnp.where(odd, far_ref[...], chip_ref[...])

    for z in range(0, QZ, 2):
        slab = depth_pair([halo_ref.at[x] for x in range(QX)], z)
        terms = jnp.dot(rim_weights[...], slab, preferred_element_type=F32)
        for h in range(2):
            rows = slice((z + h) * C, (z + h + 1) * C)
            parts = [
                partial_ref[x, rows, :]
                + taps_joined(terms[x * T3 : (x + 1) * T3, h * QY : (h + 1) * QY])
                for x in range(QX + 1)
            ]
            for x in range(QX):
                put_grad(even.at[x], odds.at[x], z + h, parts[x] * scale_ref[x, rows, :])
            partial_next[rows, :] = parts[QX]

    total = jnp.zeros((2 * T3, 256), F32)
    for z0 in range(0, QZ, 8):
        slab = jnp.concatenate(
            [
                jnp.concatenate([halo_ref[x, z * C : (z + 3) * C, :] for z in range(z0, z0 + 8)], axis=1)
                for x in range(QX)
            ],
            axis=0,
        )
        total = total + nt_dot(slab, hidden_rows(hidden_t, z0))
    second_ref[0:T3, :] = second_in[0:T3, :] + total[0:T3, 0:128]
    second_ref[T3 : 2 * T3, :] = second_in[T3 : 2 * T3, :]
    second_ref[2 * T3 :, :] = second_in[2 * T3 :, :] + total[T3:, 128:256]
    for ab in range(9):
        for d in range(3):
            begin = (ab * 3 + d) * 8
            dense_ref[1, begin : begin + 8, :] = second_row(second_ref, ab, d)

    even_sum, odd_sum = cell_sums(
        act_t, range(IX), [even.at[x] for x in range(QX)], [odds.at[x] for x in range(QX)]
    )
    even_sum, odd_sum = [
        [total[plane * T3 : (plane + 1) * T3] for plane in range(IX)] for total in (even_sum, odd_sum)
    ]
    first_ref[0, :, 0:C] = even_sum[1][:, C : 2 * C]
    first_ref[1, :, 0 : 2 * C] = odd_sum[1][:, 2 * C :]
    for side, (total, width) in enumerate(((even_sum, C), (odd_sum, 2 * C))):
        joined = jnp.concatenate(
            [total[p][:, 0:width] + total[p + 2][:, width : 2 * width] for p in range(2)], axis=0
        )
        first_flips(flips, side, joined)
    for ab in range(6):
        for d in range(3):
            begin = ((ab + 3) * 3 + d) * 8
            dense_ref[0, begin : begin + 8, :] = first_row(flips, ab, d)


def last_kernel(
    next_ref, rim_weights, partial_ref, act_t, first_ref, dense_ref,
    out_ref,
    plane, scale, even, odds, flips, head,
):
    more = lax.axis_index("space") < lax.axis_size("space") - 1
    plane[0:C, :] = jnp.zeros((C, QY), BF)
    plane[(QZ + 1) * C :, :] = jnp.zeros((2 * C, QY), BF)
    plane[C : (QZ + 1) * C, :] = next_ref[1]
    pre = next_ref[0].astype(F32)
    gate = jax.nn.sigmoid(pre)
    scale[...] = jnp.where(more, gate * (1.0 + pre * (1.0 - gate)), 0.0)

    weights = rim_weights[T3 : 2 * T3, 128:256]
    for z in range(0, QZ, 2):
        terms = jnp.dot(weights, depth_pair([plane], z), preferred_element_type=F32)
        for h in range(2):
            rows = slice((z + h) * C, (z + h + 1) * C)
            grad = partial_ref[rows, :] + taps_joined(terms[:, h * QY : (h + 1) * QY])
            put_grad(even, odds, z + h, grad * scale[rows, :])
    even_sum, odd_sum = cell_sums(act_t, [IX - 1], [even], [odds])
    first_flips(flips, 0, even_sum + first_ref[0, :, 0:C])
    first_flips(flips, 1, odd_sum + first_ref[1, :, 0 : 2 * C])
    for ab in range(3):
        for d in range(3):
            begin = (ab * 3 + d) * 8
            head[begin : begin + 8, :] = first_row(flips, ab, d)

    for s in range(16):
        begin = (27 * s) // 2
        for which in range(2):
            known = min(max(72 - begin, 0), 14) if which == 0 else 0
            begins = [head[begin : begin + known, :]] if known else []
            if known < 14:
                begins.append(dense_ref[which, begin + known : begin + 14, :])
            begins.append(jnp.zeros((2, 128), F32))
            out_ref[SHARE_ORDER.index((s, which))] = jnp.concatenate(begins, axis=0).astype(BF)


def share_kernel(shares_ref, copies_ref):
    total = shares_ref[0].astype(F32)
    for i in range(1, 32):
        total = total + shares_ref[i].astype(F32)
    for i in range(16):
        copies_ref[i] = total.astype(copies_ref.dtype)


def total_kernel(copies_ref, out_ref):
    odd = on_odd()
    lane = lax.broadcasted_iota(jnp.int32, (16, 128), 1)
    rows = []
    for which in range(2):
        first, *others = [i for i, (lane_at, _) in enumerate(COPY_ORDER) if lane_at == which]
        total = copies_ref[first].astype(F32)
        for i in others:
            total = total + copies_ref[i].astype(F32)
        turned = pltpu.roll(total, 64, 1)
        after = jnp.concatenate([turned[1:], turned[0:1]], axis=0)
        rows.append(jnp.where(odd, jnp.where(lane < 64, turned, after), total))
    for k in range(14):
        width = min(128, 1728 - 128 * k)
        both = jnp.concatenate([rows[0][k : k + 1], rows[1][k : k + 1]], axis=0)
        out_ref[:, 128 * k : 128 * k + width] = both[:, 0:width]


VMEM = pltpu.VMEM


def call(kernel, name, outs, scratch, flops, *args):
    shapes = [jax.ShapeDtypeStruct(shape, dtype) for shape, dtype in outs]
    moved = sum(a.size * a.dtype.itemsize for a in args)
    return pl.pallas_call(
        kernel,
        out_shape=shapes,
        in_specs=[pl.BlockSpec(memory_space=VMEM)] * len(args),
        out_specs=[pl.BlockSpec(memory_space=VMEM)] * len(shapes),
        scratch_shapes=scratch,
        compiler_params=pltpu.CompilerParams(vmem_limit_bytes=24 * 2**20),
        cost_estimate=pl.CostEstimate(flops=flops, bytes_accessed=moved, transcendentals=0),
        name=name,
    )(*args)


def relay(cot):
    plane = ((QZ * C, QY), BF)
    return call(
        relay_kernel,
        "relay",
        [((QX, COT_ROWS, QY), BF), plane, plane],
        [],
        10**10,
        cot,
    )


def for_prev(pre, planes):
    return call(
        prev_kernel, "for_prev", [((2, QZ * C, QY), BF)], [], 10**9, pre, planes
    )[0]


def local_terms(act, pre, weight, planes):
    return call(
        local_kernel,
        "local_terms",
        [
            ((IX, ACT_ROWS, IY), BF),
            ((QX, QZ * T3, QY), BF),
            ((QX, QZ * C, QY), F32),
            ((QX + 1, QZ * C, QY), F32),
            ((3 * T3, 256), BF),
            ((TAPS, 128), F32),
        ],
        [
            VMEM((3 * 128, 128), F32),
        ],
        5 * 10**9,
        act, pre, weight, planes,
    )


def main_terms(*args):
    return call(
        main_kernel,
        "main_terms",
        [((2, T3, 128), F32), ((2, 216, 128), F32), ((QZ * C, QY), F32)],
        [
            VMEM((QX, COT_ROWS, QY), BF),
            VMEM((QX, QZ * C, QY), BF),
            VMEM((QX, QZ * 2 * C, QY), BF),
            VMEM((TAPS, 128), F32),
            VMEM((2, T3, 128), F32),
        ],
        5 * 10**9,
        *args,
    )


def last_terms(*args):
    return call(
        last_kernel,
        "last_terms",
        [((32, 16, 128), BF)],
        [
            VMEM((COT_ROWS, QY), BF),
            VMEM((QZ * C, QY), F32),
            VMEM((QZ * C, QY), BF),
            VMEM((QZ * 2 * C, QY), BF),
            VMEM((1, T3, 128), F32),
            VMEM((72, 128), F32),
        ],
        10**9,
        *args,
    )[0]


def share_copies(shares):
    return call(share_kernel, "share_copies", [((16, 16, 128), BF)], [], 10**6, shares)[0]


def total_rows(copies):
    return call(total_kernel, "total_rows", [((2, 1728), F32)], [], 10**6, copies)[0]


def swapped(x, begin):
    pairs = []
    for i in range(begin, lax.axis_size("space") - 1, 2):
        pairs += [(i, i + 1), (i + 1, i)]
    return lax.ppermute(x, "space", pairs)


def exchanged(x, groups):
    groups = [[(s * 8 + z) * 2 + y for s, z, y in group] for group in groups]
    return lax.all_to_all(
        x, ("space", "deep", "lane"), 0, 0, axis_index_groups=groups, tiled=True
    )


def on_device(activations, preact, cotangent, conv_weight):
    act, pre, cot = activations[0], preact[0], cotangent[0]
    planes, to_chip, to_far = relay(cot)
    to_prev = for_prev(pre, planes)
    far = swapped(to_far, 1)
    after = lax.ppermute(to_prev, "space", [(i + 1, i) for i in range(lax.axis_size("space") - 1)])
    chip = swapped(to_chip, 0)
    act_t, hidden_t, scale, partial, rim_weights, second = local_terms(
        act, pre, conv_weight, planes
    )
    first, dense, partial_next = main_terms(
        far, chip, rim_weights, partial, scale, hidden_t, act_t, second
    )
    terms = last_terms(after, rim_weights, partial_next, act_t, first, dense)
    shares = exchanged(terms, [[(s, z, y) for s, y in SHARE_ORDER] for z in range(8)])
    copies = exchanged(
        share_copies(shares), [[(s, z, y) for y, z in COPY_ORDER] for s in range(16)]
    )
    return total_rows(copies)


def solution(mesh):
    split = Mesh(mesh.devices.reshape(16, 8, 2), ("space", "deep", "lane"))
    rows = P(("deep", "lane"), None, "space", None, None)
    return jax.shard_map(
        on_device,
        mesh=split,
        in_specs=(rows, rows, rows, P()),
        out_specs=P(None, "space"),
        check_vma=False,
    )
```

```python
import jax
import jax.numpy as jnp
from jax import lax
from jax.experimental import pallas as pl
from jax.experimental.pallas import tpu as pltpu
from jax.sharding import Mesh, PartitionSpec as P

BF = jnp.bfloat16
F32 = jnp.float32

C = 32
QX, QZ, QY = 2, 24, 128
IX, IZ, IY = 4, 48, 256
T3 = 3 * C
COT_ROWS = (QZ + 3) * C
ACT_ROWS = (IZ + 1) * C
TAPS = 9 * C

NT = (((1,), (1,)), ((), ()))

SHARE_ORDER = [divmod((i + 22) % 32, 2) for i in range(32)]
COPY_ORDER = [(lane, (i + 4) % 8) for lane in (1, 0) for i in range(8)]


def nt_dot(a, b):
    return lax.dot_general(a, b, NT, preferred_element_type=F32)


def lane_shift(x, by):
    lanes = lax.broadcasted_iota(jnp.int32, x.shape, 1)
    return jnp.where(lanes == (0 if by == 1 else QY - 1), 0.0, pltpu.roll(x, by % QY, 1))


def by_depth(block):
    channels, depth, last = block.shape
    return jnp.transpose(block, (1, 0, 2)).reshape(depth * channels, last)


def depth_pair(refs, z):
    return jnp.concatenate(
        [
            jnp.concatenate([ref[(z + h) * C : (z + h + 4) * C, :] for h in range(2)], axis=1)
            for ref in refs
        ],
        axis=0,
    )


def taps_joined(part):
    return part[C : 2 * C] + lane_shift(part[0:C], -1) + lane_shift(part[2 * C : T3], 1)


def four_blocks(rows):
    return jnp.concatenate([rows, rows[0:C]], axis=0)


def on_odd():
    return lax.rem(lax.axis_index("space"), 2) == 1


def relay_kernel(cot_ref, planes_ref, chip_ref, far_ref):
    odd = on_odd()
    for plane in range(QX):
        planes_ref[plane, 0:C, :] = jnp.zeros((C, QY), BF)
        planes_ref[plane, (QZ + 1) * C :, :] = jnp.zeros((2 * C, QY), BF)
    first, last = [by_depth(cot_ref[:, plane]) for plane in range(QX)]
    planes_ref[0, C : (QZ + 1) * C, :] = first
    planes_ref[1, C : (QZ + 1) * C, :] = last
    chip_ref[...] = jnp.where(odd, first, last)
    far_ref[...] = jnp.where(odd, last, first)


def flipped_weights(weight_ref, weight_t, j):
    for k in range(3):
        base = (2 - j) * 9 + (2 - k) * 3
        wide = jnp.concatenate([weight_ref[base + d].astype(F32) for d in range(3)], axis=1)
        weight_t[k * C : (k + 1) * C, 0:T3] = wide
    weight_t[3 * C :, :] = jnp.zeros((C, 128), F32)
    return weight_t[:, 0:T3].T.astype(BF)


def prev_kernel(pre_ref, planes_ref, weight_ref, prev_ref, weight_t):
    prev_ref[0] = by_depth(pre_ref[:, 0])
    odd = on_odd()

    @pl.when(odd)
    def _():
        prev_ref[1] = planes_ref[1, C : (QZ + 1) * C, :]

    @pl.when(jnp.logical_not(odd))
    def _():
        weights = flipped_weights(weight_ref, weight_t, 2)
        for z in range(0, QZ, 2):
            terms = jnp.dot(
                weights, depth_pair([planes_ref.at[1]], z), preferred_element_type=F32
            )
            for h in range(2):
                rows = slice((z + h) * C, (z + h + 1) * C)
                prev_ref[1, rows, :] = taps_joined(terms[:, h * QY : (h + 1) * QY]).astype(BF)


def hidden_rows(hidden_t, z0):
    return jnp.concatenate(
        [
            jnp.concatenate(
                [four_blocks(hidden_t[x, z * T3 : (z + 1) * T3, :]) for x in range(QX)], axis=0
            )
            for z in range(z0, z0 + 8)
        ],
        axis=1,
    )


def weight_rows(blocks):
    return jnp.concatenate([jnp.concatenate(row, axis=1) for row in blocks], axis=0)


def local_kernel(
    act_ref, pre_ref, weight_ref, planes_ref,
    act_t, hidden_t, scale_t, partial_t, rim_weights, second_ref,
    weight_t,
):
    for j in range(3):
        for k in range(3):
            base = (2 - j) * 9 + (2 - k) * 3
            wide = jnp.concatenate([weight_ref[base + d].astype(F32) for d in range(3)], axis=1)
            weight_t[(j * 4 + k) * C : (j * 4 + k + 1) * C, 0:T3] = wide
        weight_t[(j * 4 + 3) * C : (j * 4 + 4) * C, :] = jnp.zeros((C, 128), F32)
    flipped = [weight_t[j * 128 : (j + 1) * 128, 0:T3].T.astype(BF) for j in range(3)]
    none = jnp.zeros((T3, 128), BF)
    weights = weight_rows(((flipped[1], flipped[2]), (flipped[0], flipped[1]), (none, flipped[0])))
    rim_weights[...] = weight_rows(((flipped[0], none), (none, flipped[2]), (none, flipped[1])))

    for plane in range(QX):
        rows = by_depth(pre_ref[:, plane]).astype(F32)
        for z in range(QZ):
            pre = rows[z * C : (z + 1) * C]
            gate = jax.nn.sigmoid(pre)
            hidden = (pre * gate).astype(BF).astype(F32)
            hidden_t[plane, z * T3 : (z + 1) * T3, :] = jnp.concatenate(
                [lane_shift(hidden, 1), hidden, lane_shift(hidden, -1)], axis=0
            ).astype(BF)
            scale_t[plane, z * C : (z + 1) * C, :] = gate * (1.0 + pre * (1.0 - gate))

    row = lax.broadcasted_iota(jnp.int32, (IY, IY), 0)
    col = lax.broadcasted_iota(jnp.int32, (IY, IY), 1)
    split = jnp.where(row == 2 * (col % QY) + col // QY, 1.0, 0.0).astype(BF)
    for plane in range(IX):
        act_t[plane, 0:C, :] = jnp.zeros((C, IY), BF)
        rows = act_ref[:, plane].reshape(C * IZ, IY)
        rows = jnp.dot(rows, split, preferred_element_type=F32).astype(BF)
        act_t[plane, C:, :] = by_depth(rows.reshape(C, IZ, IY))

    for z in range(0, QZ, 2):
        slab = depth_pair([planes_ref.at[x] for x in range(QX)], z)
        terms = jnp.dot(weights, slab, preferred_element_type=F32)
        for x in range(QX + 1):
            for h in range(2):
                part = terms[x * T3 : (x + 1) * T3, h * QY : (h + 1) * QY]
                partial_t[x, (z + h) * C : (z + h + 1) * C, :] = taps_joined(part)

    total = jnp.zeros((2 * T3, 256), F32)
    for z0 in range(0, QZ, 8):
        slab = jnp.concatenate(
            [
                jnp.concatenate(
                    [planes_ref[x, z * C : (z + 3) * C, :] for z in range(z0, z0 + 8)], axis=1
                )
                for x in range(QX)
            ],
            axis=0,
        )
        total = total + nt_dot(slab, hidden_rows(hidden_t, z0))
    second_ref[0:T3, :] = total[0:T3, 128:256]
    second_ref[T3 : 2 * T3, :] = total[0:T3, 0:128] + total[T3:, 128:256]
    second_ref[2 * T3 :, :] = total[T3:, 0:128]


def put_grad(even_ref, odd_ref, z, grad):
    here = grad.astype(BF)
    even_ref[z * C : (z + 1) * C, :] = here
    odd_ref[2 * z * C : (2 * z + 1) * C, :] = lane_shift(grad, -1).astype(BF)
    odd_ref[(2 * z + 1) * C : (2 * z + 2) * C, :] = here


def cell_sums(act_t, planes, even_refs, odd_refs):
    totals = [0.0, 0.0]
    for z0 in range(0, QZ, 8):
        for side, (refs, step) in enumerate(((even_refs, C), (odd_refs, 2 * C))):
            lanes = slice(side * QY, (side + 1) * QY)
            acts = jnp.concatenate(
                [
                    jnp.concatenate(
                        [act_t[plane, 2 * z * C : (2 * z + 3) * C, lanes] for z in range(z0, z0 + 8)],
                        axis=1,
                    )
                    for plane in planes
                ],
                axis=0,
            )
            grads = jnp.concatenate(
                [
                    jnp.concatenate([ref[z * step : (z + 1) * step, :] for z in range(z0, z0 + 8)], axis=1)
                    for ref in refs
                ],
                axis=0,
            )
            totals[side] = totals[side] + nt_dot(acts, grads)
    return totals


def dense_row(blocks):
    lane = lax.broadcasted_iota(jnp.int32, (8, 128), 1)
    row = jnp.zeros((8, 128), F32)
    for r, (source, begin, offset) in enumerate(blocks):
        part = source[pl.ds(begin, 8, stride=4), :]
        turn = (r * C - offset) % 128
        part = pltpu.roll(part, turn, 1) if turn else part
        row = jnp.where(lane // C == r, part, row)
    return row


def second_row(source, ab, d):
    ab_rev = (2 - ab // 3) * 3 + (2 - ab % 3)
    return dense_row([(source, ab_rev * C + r, d * C) for r in range(4)])


def first_row(flips, ab, d):
    begin = (C, 0, 2 * C)[d]
    return dense_row([(flips.at[ab // 4], begin + r, (ab % 4) * C) for r in range(4)])


def first_flips(flips, side, total):
    rows = slice(0, C) if side == 0 else slice(C, T3)
    turned = total.T
    for begin in range(0, total.shape[0], 128):
        width = min(128, total.shape[0] - begin)
        flips[begin // 128, rows, 0:width] = turned[:, begin : begin + width]


def main_kernel(
    far_ref, chip_ref, rim_weights, partial_ref, scale_ref, hidden_t, act_t,
    second_in,
    first_ref, dense_ref, partial_next,
    halo_ref, even, odds, second_ref, flips,
):
    odd = on_odd()
    for x in range(QX):
        halo_ref[x, 0:C, :] = jnp.zeros((C, QY), BF)
        halo_ref[x, (QZ + 1) * C :, :] = jnp.zeros((2 * C, QY), BF)
    inner = slice(C, (QZ + 1) * C)
    halo_ref[0, inner, :] = jnp.where(odd, chip_ref[...], far_ref[...])
    halo_ref[1, inner, :] = jnp.where(odd, far_ref[...], chip_ref[...])

    for z in range(0, QZ, 2):
        slab = depth_pair([halo_ref.at[x] for x in range(QX)], z)
        terms = jnp.dot(rim_weights[...], slab, preferred_element_type=F32)
        for h in range(2):
            rows = slice((z + h) * C, (z + h + 1) * C)
            parts = [
                partial_ref[x, rows, :]
                + taps_joined(terms[x * T3 : (x + 1) * T3, h * QY : (h + 1) * QY])
                for x in range(QX + 1)
            ]
            for x in range(QX):
                put_grad(even.at[x], odds.at[x], z + h, parts[x] * scale_ref[x, rows, :])
            partial_next[rows, :] = parts[QX]

    total = jnp.zeros((2 * T3, 256), F32)
    for z0 in range(0, QZ, 8):
        slab = jnp.concatenate(
            [
                jnp.concatenate([halo_ref[x, z * C : (z + 3) * C, :] for z in range(z0, z0 + 8)], axis=1)
                for x in range(QX)
            ],
            axis=0,
        )
        total = total + nt_dot(slab, hidden_rows(hidden_t, z0))
    second_ref[0:T3, :] = second_in[0:T3, :] + total[0:T3, 0:128]
    second_ref[T3 : 2 * T3, :] = second_in[T3 : 2 * T3, :]
    second_ref[2 * T3 :, :] = second_in[2 * T3 :, :] + total[T3:, 128:256]
    for ab in range(9):
        for d in range(3):
            begin = (ab * 3 + d) * 8
            dense_ref[1, begin : begin + 8, :] = second_row(second_ref, ab, d)

    even_sum, odd_sum = cell_sums(
        act_t, range(IX), [even.at[x] for x in range(QX)], [odds.at[x] for x in range(QX)]
    )
    even_sum, odd_sum = [
        [total[plane * T3 : (plane + 1) * T3] for plane in range(IX)] for total in (even_sum, odd_sum)
    ]
    first_ref[0, :, 0:C] = even_sum[1][:, C : 2 * C]
    first_ref[1, :, 0 : 2 * C] = odd_sum[1][:, 2 * C :]
    for side, (total, width) in enumerate(((even_sum, C), (odd_sum, 2 * C))):
        joined = jnp.concatenate(
            [total[p][:, 0:width] + total[p + 2][:, width : 2 * width] for p in range(2)], axis=0
        )
        first_flips(flips, side, joined)
    for ab in range(6):
        for d in range(3):
            begin = ((ab + 3) * 3 + d) * 8
            dense_ref[0, begin : begin + 8, :] = first_row(flips, ab, d)


def last_kernel(
    next_ref, rim_weights, partial_ref, act_t, first_ref, dense_ref,
    out_ref,
    plane, scale, even, odds, flips, head,
):
    more = lax.axis_index("space") < lax.axis_size("space") - 1
    pre = next_ref[0].astype(F32)
    gate = jax.nn.sigmoid(pre)
    scale[...] = jnp.where(more, gate * (1.0 + pre * (1.0 - gate)), 0.0)

    odd = on_odd()

    @pl.when(odd)
    def _():
        for z in range(QZ):
            rows = slice(z * C, (z + 1) * C)
            grad = partial_ref[rows, :] + next_ref[1, rows, :].astype(F32)
            put_grad(even, odds, z, grad * scale[rows, :])

    @pl.when(jnp.logical_not(odd))
    def _():
        plane[0:C, :] = jnp.zeros((C, QY), BF)
        plane[(QZ + 1) * C :, :] = jnp.zeros((2 * C, QY), BF)
        plane[C : (QZ + 1) * C, :] = next_ref[1]
        weights = rim_weights[T3 : 2 * T3, 128:256]
        for z in range(0, QZ, 2):
            terms = jnp.dot(weights, depth_pair([plane], z), preferred_element_type=F32)
            for h in range(2):
                rows = slice((z + h) * C, (z + h + 1) * C)
                grad = partial_ref[rows, :] + taps_joined(terms[:, h * QY : (h + 1) * QY])
                put_grad(even, odds, z + h, grad * scale[rows, :])

    even_sum, odd_sum = cell_sums(act_t, [IX - 1], [even], [odds])
    first_flips(flips, 0, even_sum + first_ref[0, :, 0:C])
    first_flips(flips, 1, odd_sum + first_ref[1, :, 0 : 2 * C])
    for ab in range(3):
        for d in range(3):
            begin = (ab * 3 + d) * 8
            head[begin : begin + 8, :] = first_row(flips, ab, d)

    for s in range(16):
        begin = (27 * s) // 2
        for which in range(2):
            known = min(max(72 - begin, 0), 14) if which == 0 else 0
            begins = [head[begin : begin + known, :]] if known else []
            if known < 14:
                begins.append(dense_ref[which, begin + known : begin + 14, :])
            begins.append(jnp.zeros((2, 128), F32))
            out_ref[SHARE_ORDER.index((s, which))] = jnp.concatenate(begins, axis=0).astype(BF)


def share_kernel(shares_ref, copies_ref):
    total = shares_ref[0].astype(F32)
    for i in range(1, 32):
        total = total + shares_ref[i].astype(F32)
    for i in range(16):
        copies_ref[i] = total.astype(copies_ref.dtype)


def total_kernel(copies_ref, out_ref):
    odd = on_odd()
    lane = lax.broadcasted_iota(jnp.int32, (16, 128), 1)
    rows = []
    for which in range(2):
        first, *others = [i for i, (lane_at, _) in enumerate(COPY_ORDER) if lane_at == which]
        total = copies_ref[first].astype(F32)
        for i in others:
            total = total + copies_ref[i].astype(F32)
        turned = pltpu.roll(total, 64, 1)
        after = jnp.concatenate([turned[1:], turned[0:1]], axis=0)
        rows.append(jnp.where(odd, jnp.where(lane < 64, turned, after), total))
    for k in range(14):
        width = min(128, 1728 - 128 * k)
        both = jnp.concatenate([rows[0][k : k + 1], rows[1][k : k + 1]], axis=0)
        out_ref[:, 128 * k : 128 * k + width] = both[:, 0:width]


VMEM = pltpu.VMEM


def call(kernel, name, outs, scratch, flops, *args):
    shapes = [jax.ShapeDtypeStruct(shape, dtype) for shape, dtype in outs]
    moved = sum(a.size * a.dtype.itemsize for a in args)
    return pl.pallas_call(
        kernel,
        out_shape=shapes,
        in_specs=[pl.BlockSpec(memory_space=VMEM)] * len(args),
        out_specs=[pl.BlockSpec(memory_space=VMEM)] * len(shapes),
        scratch_shapes=scratch,
        compiler_params=pltpu.CompilerParams(vmem_limit_bytes=24 * 2**20),
        cost_estimate=pl.CostEstimate(flops=flops, bytes_accessed=moved, transcendentals=0),
        name=name,
    )(*args)


def relay(cot):
    plane = ((QZ * C, QY), BF)
    return call(
        relay_kernel,
        "relay",
        [((QX, COT_ROWS, QY), BF), plane, plane],
        [],
        10**10,
        cot,
    )


def for_prev(pre, planes, weight):
    return call(
        prev_kernel,
        "for_prev",
        [((2, QZ * C, QY), BF)],
        [VMEM((128, 128), F32)],
        10**9,
        pre, planes, weight,
    )[0]


def local_terms(act, pre, weight, planes):
    return call(
        local_kernel,
        "local_terms",
        [
            ((IX, ACT_ROWS, IY), BF),
            ((QX, QZ * T3, QY), BF),
            ((QX, QZ * C, QY), F32),
            ((QX + 1, QZ * C, QY), F32),
            ((3 * T3, 256), BF),
            ((TAPS, 128), F32),
        ],
        [
            VMEM((3 * 128, 128), F32),
        ],
        5 * 10**9,
        act, pre, weight, planes,
    )


def main_terms(*args):
    return call(
        main_kernel,
        "main_terms",
        [((2, T3, 128), F32), ((2, 216, 128), F32), ((QZ * C, QY), F32)],
        [
            VMEM((QX, COT_ROWS, QY), BF),
            VMEM((QX, QZ * C, QY), BF),
            VMEM((QX, QZ * 2 * C, QY), BF),
            VMEM((TAPS, 128), F32),
            VMEM((2, T3, 128), F32),
        ],
        5 * 10**9,
        *args,
    )


def last_terms(*args):
    return call(
        last_kernel,
        "last_terms",
        [((32, 16, 128), BF)],
        [
            VMEM((COT_ROWS, QY), BF),
            VMEM((QZ * C, QY), F32),
            VMEM((QZ * C, QY), BF),
            VMEM((QZ * 2 * C, QY), BF),
            VMEM((1, T3, 128), F32),
            VMEM((72, 128), F32),
        ],
        10**9,
        *args,
    )[0]


def share_copies(shares):
    return call(share_kernel, "share_copies", [((16, 16, 128), BF)], [], 10**6, shares)[0]


def total_rows(copies):
    return call(total_kernel, "total_rows", [((2, 1728), F32)], [], 10**6, copies)[0]


def swapped(x, begin):
    pairs = []
    for i in range(begin, lax.axis_size("space") - 1, 2):
        pairs += [(i, i + 1), (i + 1, i)]
    return lax.ppermute(x, "space", pairs)


def exchanged(x, groups):
    groups = [[(s * 8 + z) * 2 + y for s, z, y in group] for group in groups]
    return lax.all_to_all(
        x, ("space", "deep", "lane"), 0, 0, axis_index_groups=groups, tiled=True
    )


def on_device(activations, preact, cotangent, conv_weight):
    act, pre, cot = activations[0], preact[0], cotangent[0]
    planes, to_chip, to_far = relay(cot)
    to_prev = for_prev(pre, planes, conv_weight)
    far = swapped(to_far, 1)
    after = lax.ppermute(to_prev, "space", [(i + 1, i) for i in range(lax.axis_size("space") - 1)])
    chip = swapped(to_chip, 0)
    act_t, hidden_t, scale, partial, rim_weights, second = local_terms(
        act, pre, conv_weight, planes
    )
    first, dense, partial_next = main_terms(
        far, chip, rim_weights, partial, scale, hidden_t, act_t, second
    )
    terms = last_terms(after, rim_weights, partial_next, act_t, first, dense)
    shares = exchanged(terms, [[(s, z, y) for s, y in SHARE_ORDER] for z in range(8)])
    copies = exchanged(
        share_copies(shares), [[(s, z, y) for y, z in COPY_ORDER] for s in range(16)]
    )
    return total_rows(copies)


def solution(mesh):
    split = Mesh(mesh.devices.reshape(16, 8, 2), ("space", "deep", "lane"))
    rows = P(("deep", "lane"), None, "space", None, None)
    return jax.shard_map(
        on_device,
        mesh=split,
        in_specs=(rows, rows, rows, P()),
        out_specs=P(None, "space"),
        check_vma=False,
    )
```

```python
import jax
import jax.numpy as jnp
from jax import lax
from jax.experimental import pallas as pl
from jax.experimental.pallas import tpu as pltpu
from jax.sharding import Mesh, PartitionSpec as P

BF = jnp.bfloat16
F32 = jnp.float32

C = 32
QX, QZ, QY = 2, 24, 128
IX, IZ, IY = 4, 48, 256
T3 = 3 * C
COT_ROWS = (QZ + 3) * C
ACT_ROWS = (IZ + 1) * C
TAPS = 9 * C

NT = (((1,), (1,)), ((), ()))

SHARE_ORDER = [divmod((i + 22) % 32, 2) for i in range(32)]
COPY_ORDER = [(lane, (i + 4) % 8) for lane in (1, 0) for i in range(8)]


def nt_dot(a, b):
    return lax.dot_general(a, b, NT, preferred_element_type=F32)


def lane_shift(x, by):
    lanes = lax.broadcasted_iota(jnp.int32, x.shape, 1)
    return jnp.where(lanes == (0 if by == 1 else QY - 1), 0.0, pltpu.roll(x, by % QY, 1))


def by_depth(block):
    channels, depth, last = block.shape
    return jnp.transpose(block, (1, 0, 2)).reshape(depth * channels, last)


def depth_pair(refs, z):
    return jnp.concatenate(
        [
            jnp.concatenate([ref[(z + h) * C : (z + h + 4) * C, :] for h in range(2)], axis=1)
            for ref in refs
        ],
        axis=0,
    )


def taps_joined(part):
    return part[C : 2 * C] + lane_shift(part[0:C], -1) + lane_shift(part[2 * C : T3], 1)


def four_blocks(rows):
    return jnp.concatenate([rows, rows[0:C]], axis=0)


def on_odd():
    return lax.rem(lax.axis_index("space"), 2) == 1


def relay_kernel(cot_ref, planes_ref, chip_ref, far_ref):
    odd = on_odd()
    for plane in range(QX):
        planes_ref[plane, 0:C, :] = jnp.zeros((C, QY), BF)
        planes_ref[plane, (QZ + 1) * C :, :] = jnp.zeros((2 * C, QY), BF)
    first, last = [by_depth(cot_ref[:, plane]) for plane in range(QX)]
    planes_ref[0, C : (QZ + 1) * C, :] = first
    planes_ref[1, C : (QZ + 1) * C, :] = last
    chip_ref[...] = jnp.where(odd, first, last)
    far_ref[...] = jnp.where(odd, last, first)


def flipped_weights(weight_ref, weight_t, j):
    for k in range(3):
        base = (2 - j) * 9 + (2 - k) * 3
        wide = jnp.concatenate([weight_ref[base + d].astype(F32) for d in range(3)], axis=1)
        weight_t[k * C : (k + 1) * C, 0:T3] = wide
    weight_t[3 * C :, :] = jnp.zeros((C, 128), F32)
    return weight_t[:, 0:T3].T.astype(BF)


def prev_kernel(pre_ref, planes_ref, weight_ref, prev_ref, weight_t):
    prev_ref[0] = by_depth(pre_ref[:, 0])
    odd = on_odd()

    @pl.when(odd)
    def _():
        prev_ref[1] = planes_ref[1, C : (QZ + 1) * C, :]

    @pl.when(jnp.logical_not(odd))
    def _():
        weights = flipped_weights(weight_ref, weight_t, 2)
        for z in range(0, QZ, 2):
            terms = jnp.dot(
                weights, depth_pair([planes_ref.at[1]], z), preferred_element_type=F32
            )
            for h in range(2):
                rows = slice((z + h) * C, (z + h + 1) * C)
                prev_ref[1, rows, :] = taps_joined(terms[:, h * QY : (h + 1) * QY]).astype(BF)


def hidden_rows(hidden_t, z0):
    return jnp.concatenate(
        [
            jnp.concatenate(
                [four_blocks(hidden_t[x, z * T3 : (z + 1) * T3, :]) for x in range(QX)], axis=0
            )
            for z in range(z0, z0 + 8)
        ],
        axis=1,
    )


def weight_rows(blocks):
    return jnp.concatenate([jnp.concatenate(row, axis=1) for row in blocks], axis=0)


def local_kernel(
    act_ref, pre_ref, weight_ref, planes_ref,
    act_t, hidden_t, scale_t, partial_t, rim_weights, second_ref,
    weight_t,
):
    for j in range(3):
        for k in range(3):
            base = (2 - j) * 9 + (2 - k) * 3
            wide = jnp.concatenate([weight_ref[base + d].astype(F32) for d in range(3)], axis=1)
            weight_t[(j * 4 + k) * C : (j * 4 + k + 1) * C, 0:T3] = wide
        weight_t[(j * 4 + 3) * C : (j * 4 + 4) * C, :] = jnp.zeros((C, 128), F32)
    flipped = [weight_t[j * 128 : (j + 1) * 128, 0:T3].T.astype(BF) for j in range(3)]
    none = jnp.zeros((T3, 128), BF)
    weights = weight_rows(((flipped[1], flipped[2]), (flipped[0], flipped[1]), (none, flipped[0])))
    rim_weights[...] = weight_rows(((flipped[0], none), (none, flipped[2]), (none, flipped[1])))

    for plane in range(QX):
        rows = by_depth(pre_ref[:, plane]).astype(F32)
        for z in range(QZ):
            pre = rows[z * C : (z + 1) * C]
            gate = 0.5 + 0.5 * jnp.tanh(0.5 * pre)
            hidden = (pre * gate).astype(BF).astype(F32)
            hidden_t[plane, z * T3 : (z + 1) * T3, :] = jnp.concatenate(
                [lane_shift(hidden, 1), hidden, lane_shift(hidden, -1)], axis=0
            ).astype(BF)
            scale_t[plane, z * C : (z + 1) * C, :] = gate * (1.0 + pre * (1.0 - gate))

    row = lax.broadcasted_iota(jnp.int32, (IY, IY), 0)
    col = lax.broadcasted_iota(jnp.int32, (IY, IY), 1)
    split = jnp.where(row == 2 * (col % QY) + col // QY, 1.0, 0.0).astype(BF)
    for plane in range(IX):
        act_t[plane, 0:C, :] = jnp.zeros((C, IY), BF)
        rows = act_ref[:, plane].reshape(C * IZ, IY)
        rows = jnp.dot(rows, split, preferred_element_type=F32).astype(BF)
        act_t[plane, C:, :] = by_depth(rows.reshape(C, IZ, IY))

    for z in range(0, QZ, 2):
        slab = depth_pair([planes_ref.at[x] for x in range(QX)], z)
        terms = jnp.dot(weights, slab, preferred_element_type=F32)
        for x in range(QX + 1):
            for h in range(2):
                part = terms[x * T3 : (x + 1) * T3, h * QY : (h + 1) * QY]
                partial_t[x, (z + h) * C : (z + h + 1) * C, :] = taps_joined(part)

    total = jnp.zeros((2 * T3, 256), F32)
    for z0 in range(0, QZ, 8):
        slab = jnp.concatenate(
            [
                jnp.concatenate(
                    [planes_ref[x, z * C : (z + 3) * C, :] for z in range(z0, z0 + 8)], axis=1
                )
                for x in range(QX)
            ],
            axis=0,
        )
        total = total + nt_dot(slab, hidden_rows(hidden_t, z0))
    second_ref[0:T3, :] = total[0:T3, 128:256]
    second_ref[T3 : 2 * T3, :] = total[0:T3, 0:128] + total[T3:, 128:256]
    second_ref[2 * T3 :, :] = total[T3:, 0:128]


def put_grad(even_ref, odd_ref, z, grad):
    here = grad.astype(BF)
    even_ref[z * C : (z + 1) * C, :] = here
    odd_ref[2 * z * C : (2 * z + 1) * C, :] = lane_shift(grad, -1).astype(BF)
    odd_ref[(2 * z + 1) * C : (2 * z + 2) * C, :] = here


def cell_sums(act_t, planes, even_refs, odd_refs):
    totals = [0.0, 0.0]
    for z0 in range(0, QZ, 8):
        for side, (refs, step) in enumerate(((even_refs, C), (odd_refs, 2 * C))):
            lanes = slice(side * QY, (side + 1) * QY)
            acts = jnp.concatenate(
                [
                    jnp.concatenate(
                        [act_t[plane, 2 * z * C : (2 * z + 3) * C, lanes] for z in range(z0, z0 + 8)],
                        axis=1,
                    )
                    for plane in planes
                ],
                axis=0,
            )
            grads = jnp.concatenate(
                [
                    jnp.concatenate([ref[z * step : (z + 1) * step, :] for z in range(z0, z0 + 8)], axis=1)
                    for ref in refs
                ],
                axis=0,
            )
            totals[side] = totals[side] + nt_dot(acts, grads)
    return totals


def dense_row(blocks):
    lane = lax.broadcasted_iota(jnp.int32, (8, 128), 1)
    row = jnp.zeros((8, 128), F32)
    for r, (source, begin, offset) in enumerate(blocks):
        part = source[pl.ds(begin, 8, stride=4), :]
        turn = (r * C - offset) % 128
        part = pltpu.roll(part, turn, 1) if turn else part
        row = jnp.where(lane // C == r, part, row)
    return row


def second_row(source, ab, d):
    ab_rev = (2 - ab // 3) * 3 + (2 - ab % 3)
    return dense_row([(source, ab_rev * C + r, d * C) for r in range(4)])


def first_row(flips, ab, d):
    begin = (C, 0, 2 * C)[d]
    return dense_row([(flips.at[ab // 4], begin + r, (ab % 4) * C) for r in range(4)])


def first_flips(flips, side, total):
    rows = slice(0, C) if side == 0 else slice(C, T3)
    turned = total.T
    for begin in range(0, total.shape[0], 128):
        width = min(128, total.shape[0] - begin)
        flips[begin // 128, rows, 0:width] = turned[:, begin : begin + width]


def main_kernel(
    far_ref, chip_ref, rim_weights, partial_ref, scale_ref, hidden_t, act_t,
    second_in,
    first_ref, dense_ref, partial_next,
    halo_ref, even, odds, second_ref, flips,
):
    odd = on_odd()
    for x in range(QX):
        halo_ref[x, 0:C, :] = jnp.zeros((C, QY), BF)
        halo_ref[x, (QZ + 1) * C :, :] = jnp.zeros((2 * C, QY), BF)
    inner = slice(C, (QZ + 1) * C)
    halo_ref[0, inner, :] = jnp.where(odd, chip_ref[...], far_ref[...])
    halo_ref[1, inner, :] = jnp.where(odd, far_ref[...], chip_ref[...])

    for z in range(0, QZ, 2):
        slab = depth_pair([halo_ref.at[x] for x in range(QX)], z)
        terms = jnp.dot(rim_weights[...], slab, preferred_element_type=F32)
        for h in range(2):
            rows = slice((z + h) * C, (z + h + 1) * C)
            parts = [
                partial_ref[x, rows, :]
                + taps_joined(terms[x * T3 : (x + 1) * T3, h * QY : (h + 1) * QY])
                for x in range(QX + 1)
            ]
            for x in range(QX):
                put_grad(even.at[x], odds.at[x], z + h, parts[x] * scale_ref[x, rows, :])
            partial_next[rows, :] = parts[QX]

    total = jnp.zeros((2 * T3, 256), F32)
    for z0 in range(0, QZ, 8):
        slab = jnp.concatenate(
            [
                jnp.concatenate([halo_ref[x, z * C : (z + 3) * C, :] for z in range(z0, z0 + 8)], axis=1)
                for x in range(QX)
            ],
            axis=0,
        )
        total = total + nt_dot(slab, hidden_rows(hidden_t, z0))
    second_ref[0:T3, :] = second_in[0:T3, :] + total[0:T3, 0:128]
    second_ref[T3 : 2 * T3, :] = second_in[T3 : 2 * T3, :]
    second_ref[2 * T3 :, :] = second_in[2 * T3 :, :] + total[T3:, 128:256]
    for ab in range(9):
        for d in range(3):
            begin = (ab * 3 + d) * 8
            dense_ref[1, begin : begin + 8, :] = second_row(second_ref, ab, d)

    even_sum, odd_sum = cell_sums(
        act_t, range(IX), [even.at[x] for x in range(QX)], [odds.at[x] for x in range(QX)]
    )
    even_sum, odd_sum = [
        [total[plane * T3 : (plane + 1) * T3] for plane in range(IX)] for total in (even_sum, odd_sum)
    ]
    first_ref[0, :, 0:C] = even_sum[1][:, C : 2 * C]
    first_ref[1, :, 0 : 2 * C] = odd_sum[1][:, 2 * C :]
    for side, (total, width) in enumerate(((even_sum, C), (odd_sum, 2 * C))):
        joined = jnp.concatenate(
            [total[p][:, 0:width] + total[p + 2][:, width : 2 * width] for p in range(2)], axis=0
        )
        first_flips(flips, side, joined)
    for ab in range(6):
        for d in range(3):
            begin = ((ab + 3) * 3 + d) * 8
            dense_ref[0, begin : begin + 8, :] = first_row(flips, ab, d)


def last_kernel(
    next_ref, rim_weights, partial_ref, act_t, first_ref, dense_ref,
    out_ref,
    plane, scale, even, odds, flips, head,
):
    more = lax.axis_index("space") < lax.axis_size("space") - 1
    pre = next_ref[0].astype(F32)
    gate = 0.5 + 0.5 * jnp.tanh(0.5 * pre)
    scale[...] = jnp.where(more, gate * (1.0 + pre * (1.0 - gate)), 0.0)

    odd = on_odd()

    @pl.when(odd)
    def _():
        for z in range(QZ):
            rows = slice(z * C, (z + 1) * C)
            grad = partial_ref[rows, :] + next_ref[1, rows, :].astype(F32)
            put_grad(even, odds, z, grad * scale[rows, :])

    @pl.when(jnp.logical_not(odd))
    def _():
        plane[0:C, :] = jnp.zeros((C, QY), BF)
        plane[(QZ + 1) * C :, :] = jnp.zeros((2 * C, QY), BF)
        plane[C : (QZ + 1) * C, :] = next_ref[1]
        weights = rim_weights[T3 : 2 * T3, 128:256]
        for z in range(0, QZ, 2):
            terms = jnp.dot(weights, depth_pair([plane], z), preferred_element_type=F32)
            for h in range(2):
                rows = slice((z + h) * C, (z + h + 1) * C)
                grad = partial_ref[rows, :] + taps_joined(terms[:, h * QY : (h + 1) * QY])
                put_grad(even, odds, z + h, grad * scale[rows, :])

    even_sum, odd_sum = cell_sums(act_t, [IX - 1], [even], [odds])
    first_flips(flips, 0, even_sum + first_ref[0, :, 0:C])
    first_flips(flips, 1, odd_sum + first_ref[1, :, 0 : 2 * C])
    for ab in range(3):
        for d in range(3):
            begin = (ab * 3 + d) * 8
            head[begin : begin + 8, :] = first_row(flips, ab, d)

    for s in range(16):
        begin = (27 * s) // 2
        for which in range(2):
            known = min(max(72 - begin, 0), 14) if which == 0 else 0
            begins = [head[begin : begin + known, :]] if known else []
            if known < 14:
                begins.append(dense_ref[which, begin + known : begin + 14, :])
            begins.append(jnp.zeros((2, 128), F32))
            out_ref[SHARE_ORDER.index((s, which))] = jnp.concatenate(begins, axis=0).astype(BF)


def share_kernel(shares_ref, copies_ref):
    total = shares_ref[0].astype(F32)
    for i in range(1, 32):
        total = total + shares_ref[i].astype(F32)
    for i in range(16):
        copies_ref[i] = total.astype(copies_ref.dtype)


def total_kernel(copies_ref, out_ref):
    odd = on_odd()
    lane = lax.broadcasted_iota(jnp.int32, (16, 128), 1)
    rows = []
    for which in range(2):
        first, *others = [i for i, (lane_at, _) in enumerate(COPY_ORDER) if lane_at == which]
        total = copies_ref[first].astype(F32)
        for i in others:
            total = total + copies_ref[i].astype(F32)
        turned = pltpu.roll(total, 64, 1)
        after = jnp.concatenate([turned[1:], turned[0:1]], axis=0)
        rows.append(jnp.where(odd, jnp.where(lane < 64, turned, after), total))
    for k in range(14):
        width = min(128, 1728 - 128 * k)
        both = jnp.concatenate([rows[0][k : k + 1], rows[1][k : k + 1]], axis=0)
        out_ref[:, 128 * k : 128 * k + width] = both[:, 0:width]


VMEM = pltpu.VMEM


def call(kernel, name, outs, scratch, flops, *args):
    shapes = [jax.ShapeDtypeStruct(shape, dtype) for shape, dtype in outs]
    moved = sum(a.size * a.dtype.itemsize for a in args)
    return pl.pallas_call(
        kernel,
        out_shape=shapes,
        in_specs=[pl.BlockSpec(memory_space=VMEM)] * len(args),
        out_specs=[pl.BlockSpec(memory_space=VMEM)] * len(shapes),
        scratch_shapes=scratch,
        compiler_params=pltpu.CompilerParams(vmem_limit_bytes=24 * 2**20),
        cost_estimate=pl.CostEstimate(flops=flops, bytes_accessed=moved, transcendentals=0),
        name=name,
    )(*args)


def relay(cot):
    plane = ((QZ * C, QY), BF)
    return call(
        relay_kernel,
        "relay",
        [((QX, COT_ROWS, QY), BF), plane, plane],
        [],
        10**10,
        cot,
    )


def for_prev(pre, planes, weight):
    return call(
        prev_kernel,
        "for_prev",
        [((2, QZ * C, QY), BF)],
        [VMEM((128, 128), F32)],
        10**9,
        pre, planes, weight,
    )[0]


def local_terms(act, pre, weight, planes):
    return call(
        local_kernel,
        "local_terms",
        [
            ((IX, ACT_ROWS, IY), BF),
            ((QX, QZ * T3, QY), BF),
            ((QX, QZ * C, QY), F32),
            ((QX + 1, QZ * C, QY), F32),
            ((3 * T3, 256), BF),
            ((TAPS, 128), F32),
        ],
        [
            VMEM((3 * 128, 128), F32),
        ],
        5 * 10**9,
        act, pre, weight, planes,
    )


def main_terms(*args):
    return call(
        main_kernel,
        "main_terms",
        [((2, T3, 128), F32), ((2, 216, 128), F32), ((QZ * C, QY), F32)],
        [
            VMEM((QX, COT_ROWS, QY), BF),
            VMEM((QX, QZ * C, QY), BF),
            VMEM((QX, QZ * 2 * C, QY), BF),
            VMEM((TAPS, 128), F32),
            VMEM((2, T3, 128), F32),
        ],
        5 * 10**9,
        *args,
    )


def last_terms(*args):
    return call(
        last_kernel,
        "last_terms",
        [((32, 16, 128), BF)],
        [
            VMEM((COT_ROWS, QY), BF),
            VMEM((QZ * C, QY), F32),
            VMEM((QZ * C, QY), BF),
            VMEM((QZ * 2 * C, QY), BF),
            VMEM((1, T3, 128), F32),
            VMEM((72, 128), F32),
        ],
        10**9,
        *args,
    )[0]


def share_copies(shares):
    return call(share_kernel, "share_copies", [((16, 16, 128), BF)], [], 10**6, shares)[0]


def total_rows(copies):
    return call(total_kernel, "total_rows", [((2, 1728), F32)], [], 10**6, copies)[0]


def swapped(x, begin):
    pairs = []
    for i in range(begin, lax.axis_size("space") - 1, 2):
        pairs += [(i, i + 1), (i + 1, i)]
    return lax.ppermute(x, "space", pairs)


def exchanged(x, groups):
    groups = [[(s * 8 + z) * 2 + y for s, z, y in group] for group in groups]
    return lax.all_to_all(
        x, ("space", "deep", "lane"), 0, 0, axis_index_groups=groups, tiled=True
    )


def on_device(activations, preact, cotangent, conv_weight):
    act, pre, cot = activations[0], preact[0], cotangent[0]
    planes, to_chip, to_far = relay(cot)
    to_prev = for_prev(pre, planes, conv_weight)
    far = swapped(to_far, 1)
    after = lax.ppermute(to_prev, "space", [(i + 1, i) for i in range(lax.axis_size("space") - 1)])
    chip = swapped(to_chip, 0)
    act_t, hidden_t, scale, partial, rim_weights, second = local_terms(
        act, pre, conv_weight, planes
    )
    first, dense, partial_next = main_terms(
        far, chip, rim_weights, partial, scale, hidden_t, act_t, second
    )
    terms = last_terms(after, rim_weights, partial_next, act_t, first, dense)
    shares = exchanged(terms, [[(s, z, y) for s, y in SHARE_ORDER] for z in range(8)])
    copies = exchanged(
        share_copies(shares), [[(s, z, y) for y, z in COPY_ORDER] for s in range(16)]
    )
    return total_rows(copies)


def solution(mesh):
    split = Mesh(mesh.devices.reshape(16, 8, 2), ("space", "deep", "lane"))
    rows = P(("deep", "lane"), None, "space", None, None)
    return jax.shard_map(
        on_device,
        mesh=split,
        in_specs=(rows, rows, rows, P()),
        out_specs=P(None, "space"),
        check_vma=False,
    )
```
